32 devices in a mesh: rows: 4 (over y, core), band: 8 (over z, x).
Axes of the slice: x: 2, y: 2, z: 4, core: 2. Of those that a mesh axis runs over, the one named last changes fastest.
Arguments:
- patches: bfloat16 [24, 256, 3072], P('rows', None, 'band'), may hold values from -6 to 6
- condition_table: bfloat16 [64, 384], replicated, may hold values from -6 to 6
- condition_index: int32 [24, 8], P('rows'), may hold values from 0 to 63
- image_lengths: int32 [24, 8], P('rows'), may hold values from 0 to 1024, as said below
- modulate_weight: bfloat16 [384, 2304], replicated, may hold values from -0.3125 to 0.3125
- modulate_bias: bfloat16 [2304], replicated, may hold values from -3 to 3
- triple_weight: bfloat16 [384, 1152], replicated, may hold values from -0.3125 to 0.3125
- query_bias: bfloat16 [384], replicated, may hold values from -3 to 3
- value_bias: bfloat16 [384], replicated, may hold values from -3 to 3
- mixer_weight: bfloat16 [384, 384], replicated, may hold values from -3.5 to 3.5
- mixer_bias: bfloat16 [384], replicated, may hold values from -3 to 3
- hidden_weight: bfloat16 [384, 1536], replicated, may hold values from -0.3125 to 0.3125
- hidden_bias: bfloat16 [1536], replicated, may hold values from -3 to 3
- output_weight: bfloat16 [1536, 384], replicated, may hold values from -0.15625 to 0.15625
- output_bias: bfloat16 [384], replicated, may hold values from -3 to 3
- cotangent: bfloat16 [24, 256, 3072], P('rows', None, 'band'), may hold values from -6 to 6
Outputs:
- block_out: bfloat16 [24, 256, 3072], P('rows', None, 'band')
- patch_grad: float32 [24, 256, 3072], P('rows', None, 'band')
- modulate_weight_grad: float32 [384, 2304], replicated
- modulate_bias_grad: float32 [2304], replicated
- triple_weight_grad: float32 [384, 1152], replicated
- query_bias_grad: float32 [384], replicated
- value_bias_grad: float32 [384], replicated
- mixer_weight_grad: float32 [384, 384], replicated
- mixer_bias_grad: float32 [384], replicated
- hidden_weight_grad: float32 [384, 1536], replicated
- hidden_bias_grad: float32 [1536], replicated
- output_weight_grad: float32 [1536, 384], replicated
- output_bias_grad: float32 [384], replicated
The draws below stay inside these ranges and needn't reach their ends.
Inputs may be any that keep to these rules, and one draw needn't show every extreme that they name: `image_lengths`: in each row the nonzero lengths are 1024 or 256 and add up to 2048; they fill the first slots, the remaining slots of the 8 are zero.
All inputs are finite; a program needn't handle non-finite values.
Results may differ from the reference program's by a relative error of at most 0.014.
The reference program's roundings to bfloat16 on the way count: a program that leaves them out, or rounds other values in their place, can miss the bound.
Values may be sent and summed in bfloat16 or wider, within the bound.
No kernel may reach another device: no remote copies, remote signals or barrier semaphores. Data moves between devices by JAX's collectives and lax.ppermute only.
A program may use at most 128 MiB of HBM per device.

```python
import jax
import jax.numpy as jnp
from jax import lax

D = 384
HEADS = 6
HEAD_DIM = 64
FF = 1536
NCOND = 64
SEGS = 8
ROW_LEN = 2048
BAND_LEN = 256
ROWS = 24
N_BAND = 8


def draw_image_lengths(key, part):
    key = jax.random.fold_in(key, 11)
    big_key, turn_key = jax.random.split(key)
    row_ids = jnp.arange(ROWS, dtype=jnp.int32)
    big_count = jax.random.randint(big_key, (ROWS,), 0, 3, dtype=jnp.int32)
    big_count = jnp.where(row_ids == 0, 1, big_count)
    image_count = big_count + (2 - big_count) * 4
    slot_ids = jnp.arange(SEGS, dtype=jnp.int32)[None, :]
    ordered = jnp.where(slot_ids < big_count[:, None], ROW_LEN // 2, jnp.where(slot_ids < image_count[:, None], ROW_LEN // 8, 0))
    turns = jax.random.randint(turn_key, (ROWS,), 0, 8, dtype=jnp.int32) % image_count
    source = jnp.where(slot_ids < image_count[:, None], (slot_ids + turns[:, None]) % image_count[:, None], slot_ids)
    return jnp.take_along_axis(ordered, source.astype(jnp.int32), axis=1).astype(jnp.int32)


def plant(drawn, rng, smallest, high):
    longest = drawn.shape.index(max(drawn.shape))
    spots = []
    for shift in (0, 1):
        where = [jax.random.randint(jax.random.fold_in(rng, axis), (), 0, length) for axis, length in enumerate(drawn.shape)]
        where[longest] = (where[longest] + shift) % drawn.shape[longest]
        spots.append(tuple(where))
    return drawn.at[spots[0]].set(smallest).at[spots[1]].set(high)


def shard_levels(key, extent, cuts, least, high):
    loudness = 1.0
    for position, parts in cuts:
        heights = jax.random.uniform(jax.random.fold_in(jax.random.fold_in(key, 6), position), (parts,), jnp.float32, least / len(cuts), high / len(cuts))
        loudness = loudness * jnp.repeat(jnp.exp(heights), extent[position] // parts).reshape((-1,) + (1,) * (len(extent) - 1 - position))
    return loudness


def noise(stream_key, dims, deviation, bound, pieces=(), kind=jnp.bfloat16):
    values = jax.random.normal(stream_key, dims, jnp.float32) * deviation
    if len(pieces) > 0:
        values = shard_levels(stream_key, dims, pieces, -0.22, 0.18) * values
    return jnp.clip(values, min=-bound, max=bound).astype(kind)


def setup_inputs(seed: int = 0) -> dict:
    seeds = jax.random.split(jax.random.key(seed), 17)
    patches = noise(seeds[0], (ROWS, BAND_LEN, N_BAND * D), 1.0, 6.0, ((0, 4), (2, 8)))
    condition_table = noise(seeds[1], (NCOND, D), 1.0, 6.0)
    condition_index = plant(jax.random.randint(seeds[2], (ROWS, SEGS), 0, NCOND), jax.random.fold_in(seeds[2], 1), 0, NCOND - 1).astype(jnp.int32)
    image_lengths = draw_image_lengths(jax.random.fold_in(seeds[16], 71), 0)
    modulate_weight = noise(seeds[4], (D, 6 * D), D ** -0.5, 0.3125)
    modulate_bias = noise(seeds[5], (6 * D,), 0.5, 3.0)
    triple_weight = noise(seeds[6], (D, 3 * D), D ** -0.5, 0.3125)
    query_bias = noise(seeds[7], (D,), 0.5, 3.0)
    value_bias = noise(seeds[8], (D,), 0.5, 3.0)
    mixer_weight = noise(seeds[9], (D, D), (max(D // 128, 1)) ** -0.5, 3.5)
    mixer_bias = noise(seeds[10], (D,), 0.5, 3.0)
    hidden_weight = noise(seeds[11], (D, FF), D ** -0.5, 0.3125)
    hidden_bias = noise(seeds[12], (FF,), 0.5, 3.0)
    output_weight = noise(seeds[13], (FF, D), FF ** -0.5, 0.15625)
    output_bias = noise(seeds[14], (D,), 0.5, 3.0)
    cotangent = noise(seeds[15], (ROWS, BAND_LEN, N_BAND * D), 1.0, 6.0, ((0, 4), (2, 8)))
    return {"patches": patches, "condition_table": condition_table, "condition_index": condition_index, "image_lengths": image_lengths, "modulate_weight": modulate_weight, "modulate_bias": modulate_bias, "triple_weight": triple_weight, "query_bias": query_bias, "value_bias": value_bias, "mixer_weight": mixer_weight, "mixer_bias": mixer_bias, "hidden_weight": hidden_weight, "hidden_bias": hidden_bias, "output_weight": output_weight, "output_bias": output_bias, "cotangent": cotangent}


@jax.custom_vjp
def low(v):
    return lax.optimization_barrier(v.astype(jnp.bfloat16)).astype(jnp.float32)

@jax.custom_vjp
def low_back(v):
    return v

def low_keep(v):
    return (low(v), None)

def low_pass(kept, grad):
    return (grad,)

def back_keep(v):
    return (v, None)

def back_low(kept, grad):
    return (low(grad),)
low.defvjp(low_keep, low_pass)
low_back.defvjp(back_keep, back_low)
EPSILON = 1e-06
HIGHEST = lax.Precision.HIGHEST

def matmul(left, right):
    return jnp.dot(left, right, preferred_element_type=jnp.float32, precision=HIGHEST)

def layer_norm(values):
    centre = values - lax.optimization_barrier(jnp.mean(values, axis=-1, keepdims=True))
    return centre * lax.rsqrt(lax.optimization_barrier(jnp.mean(centre * centre, axis=-1, keepdims=True)) + EPSILON)

def attention(query, keys, values, segment):
    length = query.shape[0]
    query_heads = query.reshape(length, HEADS, HEAD_DIM).transpose(1, 0, 2)
    key_heads = keys.reshape(length, HEADS, HEAD_DIM).transpose(1, 0, 2)
    value_heads = values.reshape(length, HEADS, HEAD_DIM).transpose(1, 0, 2)
    scores = low_back(jnp.einsum('hqd,hkd->hqk', query_heads, key_heads, precision=HIGHEST) * HEAD_DIM ** (-0.5))
    same_image = segment[:, None] == segment[None, :]
    scores = jnp.where(same_image[None], scores, -1e+30)
    maxima = lax.optimization_barrier(jnp.max(scores, axis=2, keepdims=True))
    exps = jnp.exp(scores - maxima)
    probs = low(exps / lax.optimization_barrier(jnp.sum(exps, axis=2, keepdims=True)))
    mixed = jnp.einsum('hqk,hkd->hqd', probs, value_heads, precision=HIGHEST)
    return mixed.transpose(1, 0, 2).reshape(length, HEADS * HEAD_DIM)

def forward(params, row_input, condition_rows, segment):
    modulate_weight, modulate_bias, triple_weight, query_bias, value_bias, mixer_weight, mixer_bias, hidden_weight, hidden_bias, output_weight, output_bias = params
    activity = low(jax.nn.silu(condition_rows))
    modulation = matmul(activity, modulate_weight) + modulate_bias
    per_patch = modulation[segment]
    shift_one, scale_one, gate_one, shift_two, scale_two, gate_two = jnp.split(per_patch, 6, axis=1)
    normed_in = low(layer_norm(row_input) * (1.0 + scale_one) + shift_one)
    triple = matmul(normed_in, triple_weight)
    query = low_back(low(triple[:, :D] + query_bias))
    keys = low_back(low(triple[:, D:2 * D]))
    values = low_back(low(triple[:, 2 * D:] + value_bias))
    mixed = low_back(low(jax.checkpoint(attention)(query, keys, values, segment)))
    branch = low_back(matmul(mixed, mixer_weight) + mixer_bias)
    middle = row_input + gate_one * branch
    normed_mid = low(layer_norm(middle) * (1.0 + scale_two) + shift_two)
    hidden = low_back(matmul(normed_mid, hidden_weight) + hidden_bias)
    active = low(jax.nn.gelu(hidden, approximate=True))
    output = low_back(matmul(active, output_weight) + output_bias)
    return middle + gate_two * output

def reference(patches, condition_table, condition_index, image_lengths, modulate_weight, modulate_bias, triple_weight, query_bias, value_bias, mixer_weight, mixer_bias, hidden_weight, hidden_bias, output_weight, output_bias, cotangent):
    params = tuple((weight.astype(jnp.float32) for weight in (modulate_weight, modulate_bias, triple_weight, query_bias, value_bias, mixer_weight, mixer_bias, hidden_weight, hidden_bias, output_weight, output_bias)))
    cond_matrix = condition_table.astype(jnp.float32)
    inputs = patches.astype(jnp.float32).reshape(ROWS, BAND_LEN, N_BAND, D).reshape(ROWS, ROW_LEN, D)
    grads_in = cotangent.astype(jnp.float32).reshape(ROWS, BAND_LEN, N_BAND, D).reshape(ROWS, ROW_LEN, D)
    positions = jnp.arange(ROW_LEN, dtype=jnp.int32)

    def one_row(totals, row_items):
        row_input, row_grad, row_index, row_lengths = row_items
        row_ends = jnp.cumsum(row_lengths).astype(jnp.int32)
        segment = lax.optimization_barrier(jnp.sum((positions[:, None] >= row_ends[None, :]).astype(jnp.int32), axis=1)).astype(jnp.int32)
        condition_rows = cond_matrix[row_index]
        result, pullback = jax.vjp(lambda weights, source: forward(weights, source, condition_rows, segment), params, row_input)
        weight_grads, input_grad = pullback(row_grad)
        totals = jax.tree.map(lambda summed, addend: summed + addend, totals, weight_grads)
        return (totals, (result, input_grad))
    zeros = jax.tree.map(jnp.zeros_like, params)
    totals, (results, input_grads) = lax.scan(one_row, zeros, (inputs, grads_in, condition_index, image_lengths))
    block_out = results.reshape(ROWS, BAND_LEN, N_BAND * D).astype(jnp.bfloat16)
    patch_grad = input_grads.reshape(ROWS, BAND_LEN, N_BAND * D)
    return (block_out, patch_grad, totals[0], totals[1], totals[2], totals[3], totals[4], totals[5], totals[6], totals[7], totals[8], totals[9], totals[10])
```

```python
from functools import partial

import jax
import jax.numpy as jnp
from jax import lax
from jax.experimental import pallas as pl
from jax.experimental.pallas import tpu as pltpu
from jax.sharding import PartitionSpec as P

HEADS = 6
HEAD_DIM = 64
PAIRS = HEADS // 2
LANES = 128
BLOCK = 256
HALF = 4
EPSILON = 1e-06
ONES = 16
F32 = jnp.float32
BF16 = jnp.bfloat16
MIB = 1 << 20


def dot(left, right):
    return jnp.dot(left, right, preferred_element_type=F32)


def dot_nt(left, right):
    return lax.dot_general(left, right, (((1,), (1,)), ((), ())), preferred_element_type=F32)


def params(limit=56, **more):
    return pltpu.CompilerParams(vmem_limit_bytes=limit * MIB, **more)


def full(shape):
    return pl.BlockSpec(shape, lambda *_: (0,) * len(shape))


SMEM = pl.BlockSpec(memory_space=pltpu.SMEM)


def row_layout(lens_ref, row, slots, big):
    count = jnp.int32(0)
    before = jnp.int32(0)
    for j in range(slots):
        is_big = (lens_ref[row, j] == big).astype(jnp.int32)
        before = before + jnp.where(count + is_big == 0, 1, 0)
        count = count + is_big
    return count, jnp.where(count == 1, before, 0)


def chunk_of(start, half, k):
    return jnp.where(half == 0, start + k, jnp.where(k < start, k, k + HALF))


class Plan:
    def __init__(self, rows, bands):
        self.rows, self.bands = rows, bands
        self.halves = 2 * rows
        self.whole = self.halves // bands
        assert self.whole <= 1
        self.rest = self.halves - self.whole * bands
        self.group = 1
        while self.rest and self.rest * self.group * 2 <= bands and self.group < HALF:
            self.group *= 2
        self.idle = self.rest * self.group != bands
        self.own = HALF // self.group

    def units(self):
        found = []
        if self.whole:
            found.append(("whole", HALF))
        if self.rest:
            found.append(("shared", self.own))
        return found

    def half_row(self, name, device):
        if name == "whole":
            return device
        return self.whole * self.bands + device // self.group

    def first(self, name, device):
        return 0 if name == "whole" else (device % self.group) * self.own


def pack_kernel(plan, chunk, slots, big, me_ref, lens_ref, x_ref, *outs):
    me = me_ref[0]
    at = 0
    for name, count in plan.units():
        for s in range(plan.bands):
            dest = me ^ s
            half_row = jnp.minimum(plan.half_row(name, dest), plan.halves - 1)
            row, half = half_row // 2, half_row % 2
            start = row_layout(lens_ref, row, slots, big)[1]
            for k in range(count):
                source = chunk_of(start, half, plan.first(name, dest) + k)
                outs[at][k] = x_ref[row, pl.ds(pl.multiple_of(source * chunk, chunk), chunk), :]
            at += 1


def pack(plan, chunk, big, me, lens, x):
    width = x.shape[2]
    shapes = [
        jax.ShapeDtypeStruct((count, chunk, width), x.dtype)
        for _, count in plan.units()
        for _ in range(plan.bands)
    ]
    return pl.pallas_call(
        partial(pack_kernel, plan, chunk, lens.shape[1], big),
        in_specs=[SMEM, SMEM, full(x.shape)],
        out_specs=[full(s.shape) for s in shapes],
        out_shape=shapes,
        grid=(1,),
        compiler_params=params(32),
        name="pack",
    )(me, lens, x)


def unpack_kernel(plan, chunk, slots, big, me_ref, lens_ref, *refs):
    out_ref = refs[-1]
    me = me_ref[0]
    at = 0
    for name, count in plan.units():
        for s in range(plan.bands):
            owner = me ^ s
            half_row = plan.half_row(name, owner)

            def place(piece=refs[at], name=name, count=count, owner=owner, half_row=half_row):
                row, half = half_row // 2, half_row % 2
                start = row_layout(lens_ref, row, slots, big)[1]
                for k in range(count):
                    source = chunk_of(start, half, plan.first(name, owner) + k)
                    rows = pl.ds(pl.multiple_of(source * chunk, chunk), chunk)
                    out_ref[row, rows, :] = piece[k].astype(out_ref.dtype)

            if name == "shared" and plan.idle:
                pl.when(half_row < plan.halves)(place)
            else:
                place()
            at += 1


def unpack(plan, chunk, big, me, lens, pieces, dtype):
    width = pieces[0].shape[2]
    shape = (plan.rows, chunk * 2 * HALF, width)
    return pl.pallas_call(
        partial(unpack_kernel, plan, chunk, lens.shape[1], big),
        in_specs=[SMEM, SMEM] + [full(p.shape) for p in pieces],
        out_specs=full(shape),
        out_shape=jax.ShapeDtypeStruct(shape, dtype),
        grid=(1,),
        compiler_params=params(32),
        name="unpack",
    )(me, lens, *pieces)


def layer_norm(values):
    centre = values - jnp.mean(values, axis=-1, keepdims=True)
    inverse = lax.rsqrt(jnp.mean(centre * centre, axis=-1, keepdims=True) + EPSILON)
    return centre * inverse, inverse


def norm_back(grad, normed, inverse):
    return inverse * (
        grad
        - jnp.mean(grad, axis=-1, keepdims=True)
        - normed * jnp.mean(grad * normed, axis=-1, keepdims=True)
    )


def column_sum(values):
    return jnp.sum(values, axis=0, keepdims=True)


def attend_kernel(n, nq, nk, chunk, width, flag_ref, *refs):
    pieces, refs = refs[:n], refs[n:]
    count = nk // nq - 1
    others, refs = refs[:count], refs[count:]
    mods_ref, weight_ref, query_bias_ref, value_bias_ref = refs[:4]
    x_out, hin_out, q_out, k_out, v_out, e_out, ot_out, inv_out, mixed_out = refs[4:13]
    k_scr, qt_scr, vt_scr = refs[13:]
    p = pl.program_id(0)

    @pl.when(p == 0)
    def _():
        qt_scr[...] = jnp.zeros_like(qt_scr)
        for h in range(HEADS):
            vt_scr[h, HEAD_DIM:, :] = jnp.ones((ONES, nk * BLOCK), BF16)
        for b in range(nk):
            rows = pl.ds(b * BLOCK, BLOCK)
            if b < nq:
                for s in range(n):
                    x_out[pl.ds(b * BLOCK + s * chunk, chunk), :] = pieces[s][b]
            else:
                t, inner = b // nq - 1, b % nq
                x_out[rows, :] = others[t][pl.ds(inner * BLOCK, BLOCK), :]
            source = x_out[rows, :].astype(F32)
            normed = layer_norm(source)[0]
            shift = mods_ref[b : b + 1, 0:width]
            scale = mods_ref[b : b + 1, width : 2 * width]
            hin = (normed * (1.0 + scale) + shift).astype(BF16)
            hin_out[rows, :] = hin
            triple = dot(hin, weight_ref[...])
            keys = triple[:, width : 2 * width].astype(BF16)
            values = (triple[:, 2 * width :] + value_bias_ref[...]).astype(BF16)
            values_t = values.T
            for j in range(PAIRS):
                lanes = slice(j * LANES, (j + 1) * LANES)
                k_scr[j, rows, :] = keys[:, lanes]
                k_out[j, rows, :] = keys[:, lanes]
                v_out[j, rows, :] = values[:, lanes]
            for h in range(HEADS):
                vt_scr[h, :HEAD_DIM, rows] = values_t[h * HEAD_DIM : (h + 1) * HEAD_DIM]
            if b < nq:
                query = (triple[:, :width] + query_bias_ref[...]) * (HEAD_DIM**-0.5)
                query = query.astype(BF16)
                for j in range(PAIRS):
                    q_out[j, rows, :] = query[:, j * LANES : (j + 1) * LANES]
                query_t = query.T
                for h in range(HEADS):
                    to = (h % 2) * HEAD_DIM
                    qt_scr[h, to : to + HEAD_DIM, rows] = query_t[
                        h * HEAD_DIM : (h + 1) * HEAD_DIM
                    ]

    def tile(qt, low, size):
        columns = pl.ds(pl.multiple_of(qt * BLOCK, BLOCK), BLOCK)
        krows = pl.ds(low, size)
        found = []
        for hh in range(2):
            h = 2 * p + hh
            scores = dot(k_scr[p, krows, :], qt_scr[h, :, columns])
            exps = jnp.exp(scores - jnp.max(scores, axis=0, keepdims=True)).astype(BF16)
            e_out[hh, krows, columns] = exps
            summed = dot(vt_scr[h, :, krows], exps)
            inverse = 1.0 / summed[HEAD_DIM : HEAD_DIM + 1]
            found.append(summed[:HEAD_DIM] * inverse)
            inv_out[0, hh : hh + 1, columns] = inverse
        both = jnp.concatenate(found, axis=0)
        ot_out[0, :, columns] = both
        mixed_out[columns, :] = both.T.astype(BF16)

    @pl.when(flag_ref[0] == 1)
    def _():
        @pl.loop(0, nq)
        def _(qt):
            tile(qt, 0, nk * BLOCK)

    @pl.when(flag_ref[0] == 0)
    def _():
        @pl.loop(0, nq)
        def _(qt):
            tile(qt, pl.multiple_of(qt * BLOCK, BLOCK), BLOCK)


def attend(n, nq, nk, chunk, flag, pieces, others, mods, weight, query_bias, value_bias):
    width = weight.shape[0]
    qs, ks = nq * BLOCK, nk * BLOCK
    shape = jax.ShapeDtypeStruct
    outs = [
        (shape((ks, width), BF16), None),
        (shape((ks, width), BF16), None),
        (shape((PAIRS, qs, LANES), BF16), None),
        (shape((PAIRS, ks, LANES), BF16), None),
        (shape((PAIRS, ks, LANES), BF16), None),
        (shape((HEADS, ks, qs), BF16), pl.BlockSpec((2, ks, qs), lambda p: (p, 0, 0))),
        (shape((PAIRS, LANES, qs), F32), pl.BlockSpec((1, LANES, qs), lambda p: (p, 0, 0))),
        (shape((PAIRS, 8, qs), F32), pl.BlockSpec((1, 8, qs), lambda p: (p, 0, 0))),
        (shape((qs, width), BF16), pl.BlockSpec((qs, LANES), lambda p: (0, p))),
    ]
    arrays = [*pieces, *others, mods, weight, query_bias, value_bias]
    flops = 2 * ks * width * 3 * width + 4 * HEADS * qs * ks * HEAD_DIM * 4
    return pl.pallas_call(
        partial(attend_kernel, n, nq, nk, chunk, width),
        grid=(PAIRS,),
        in_specs=[SMEM] + [full(a.shape) for a in arrays],
        out_specs=[spec or full(s.shape) for s, spec in outs],
        out_shape=[s for s, _ in outs],
        scratch_shapes=[
            pltpu.VMEM((PAIRS, ks, LANES), BF16),
            pltpu.VMEM((HEADS, LANES, qs), BF16),
            pltpu.VMEM((HEADS, HEAD_DIM + ONES, ks), BF16),
        ],
        compiler_params=params(),
        cost_estimate=pl.CostEstimate(
            flops=flops, bytes_accessed=2 * HEADS * qs * ks, transcendentals=HEADS * qs * ks
        ),
        name="attend",
    )(flag, *arrays)


def attend_back_kernel(nq, nk, width, flag_ref, *refs):
    e_ref, q_ref, k_ref, v_ref, ot_ref, inv_ref, grad_ref, hin_ref, weight_ref = refs[:9]
    count = nk // nq - 1
    own_out, others_out = refs[9], refs[10 : 10 + count]
    tw_out, tb_out, dk_acc, dv_acc, kt_scr, tg_scr = refs[10 + count :]
    p = pl.program_id(0)
    dk_acc[...] = jnp.zeros_like(dk_acc)
    dv_acc[...] = jnp.zeros_like(dv_acc)
    kt_scr[...] = k_ref[0].T
    lane = lax.broadcasted_iota(jnp.int32, (BLOCK, LANES), 1)

    if nk > nq:

        @pl.when(p == 0)
        def _():
            tg_scr[0, nq * BLOCK :, :] = jnp.zeros(((nk - nq) * BLOCK, LANES), BF16)
            tg_scr[1, nq * BLOCK :, :] = jnp.zeros(((nk - nq) * BLOCK, LANES), BF16)
            tg_scr[2, nq * BLOCK :, :] = jnp.zeros(((nk - nq) * BLOCK, LANES), BF16)

    def tile(qt, low, size):
        columns = pl.ds(pl.multiple_of(qt * BLOCK, BLOCK), BLOCK)
        krows = pl.ds(low, size)
        grad_t = grad_ref[columns, :].astype(F32).T
        query = q_ref[0, columns, :]
        zeros = jnp.zeros((HEAD_DIM, BLOCK), BF16)
        found = []
        for hh in range(2):
            part = slice(hh * HEAD_DIM, (hh + 1) * HEAD_DIM)
            scaled = (grad_t[part] * inv_ref[0, hh : hh + 1, columns]).astype(BF16)
            delta = column_sum(scaled.astype(F32) * ot_ref[0, part, columns])
            masked = jnp.concatenate([scaled, zeros] if hh == 0 else [zeros, scaled], axis=0)
            exps = e_ref[hh, krows, columns]
            prob_grad = dot(v_ref[0, krows, :], masked)
            score_grad = (exps.astype(F32) * (prob_grad - delta)).astype(BF16)
            dv_acc[krows, :] += dot_nt(exps, masked)
            own = (lane < HEAD_DIM) if hh == 0 else (lane >= HEAD_DIM)
            dk_acc[krows, :] += dot(score_grad, jnp.where(own, query, jnp.zeros_like(query)))
            found.append(dot(kt_scr[part, krows], score_grad))
        both = jnp.concatenate(found, axis=0) * (HEAD_DIM**-0.5)
        tg_scr[p, columns, :] = both.T.astype(BF16)

    @pl.when(flag_ref[0] == 1)
    def _():
        @pl.loop(0, nq)
        def _(qt):
            tile(qt, 0, nk * BLOCK)

    @pl.when(flag_ref[0] == 0)
    def _():
        @pl.loop(0, nq)
        def _(qt):
            tile(qt, pl.multiple_of(qt * BLOCK, BLOCK), BLOCK)

    tg_scr[PAIRS + p] = dk_acc[...].astype(BF16)
    tg_scr[2 * PAIRS + p] = dv_acc[...].astype(BF16)

    @pl.when(p == PAIRS - 1)
    def _():
        grads = jnp.concatenate([tg_scr[j] for j in range(3 * PAIRS)], axis=1)
        back = dot_nt(grads, weight_ref[...])
        own_out[...] = back[: nq * BLOCK]
        for t in range(count):
            lo = (t + 1) * nq * BLOCK
            others_out[t][...] = back[lo : lo + nq * BLOCK].astype(BF16)
        tw_out[...] = dot(hin_ref[...].T, grads)
        tb_out[...] = jnp.broadcast_to(column_sum(grads.astype(F32)), tb_out.shape)


def attend_back(nq, nk, flag, kept, grad, weight):
    hin, q, k, v, e, ot, inv = kept
    width = weight.shape[0]
    qs, ks = nq * BLOCK, nk * BLOCK
    shape = jax.ShapeDtypeStruct
    outs = [shape((qs, width), F32)]
    outs += [shape((qs, width), BF16)] * (nk // nq - 1)
    outs += [shape((width, 3 * width), F32), shape((8, 3 * width), F32)]
    by_pair = lambda *tail: pl.BlockSpec((1,) + tail, lambda p: (p, 0, 0))
    flops = 4 * ks * width * 3 * width + 8 * HEADS * qs * ks * HEAD_DIM * 4
    return pl.pallas_call(
        partial(attend_back_kernel, nq, nk, width),
        grid=(PAIRS,),
        in_specs=[
            SMEM,
            pl.BlockSpec((2, ks, qs), lambda p: (p, 0, 0)),
            by_pair(qs, LANES),
            by_pair(ks, LANES),
            by_pair(ks, LANES),
            by_pair(LANES, qs),
            by_pair(8, qs),
            pl.BlockSpec((qs, LANES), lambda p: (0, p)),
            full(hin.shape),
            full(weight.shape),
        ],
        out_specs=[full(s.shape) for s in outs],
        out_shape=outs,
        scratch_shapes=[
            pltpu.VMEM((ks, LANES), F32),
            pltpu.VMEM((ks, LANES), F32),
            pltpu.VMEM((LANES, ks), BF16),
            pltpu.VMEM((3 * PAIRS, ks, LANES), BF16),
        ],
        compiler_params=params(),
        cost_estimate=pl.CostEstimate(
            flops=flops, bytes_accessed=2 * HEADS * qs * ks, transcendentals=0
        ),
        name="attend_back",
    )(flag, e, q, k, v, ot, inv, grad, hin, weight)


SMALL = 16


def feed_kernel(units, n, chunk, width, valid_ref, *refs):
    total = sum(count for _, count in units)
    u = len(units)
    xs, mixes, refs = refs[:u], refs[u : 2 * u], refs[2 * u :]
    cots, refs = [refs[i * n : (i + 1) * n] for i in range(u)], refs[u * n :]
    mods_ref, mixer_w, mixer_b, hidden_w, hidden_b, output_w, output_b = refs[:7]
    refs = refs[7:]
    outs, refs = [refs[i * n : (i + 1) * n] for i in range(u)], refs[u * n :]
    middle_out, mixed_grad_out, grads_out, slots_out = refs[:4]
    x_scr, mix_scr, cot_scr, ow_acc, hw_acc, mw_acc, ob_acc, hb_acc, mb_acc = refs[4:]
    i = pl.program_id(0)

    @pl.when(i == 0)
    def _():
        for acc in (ow_acc, hw_acc, mw_acc, ob_acc, hb_acc, mb_acc):
            acc[...] = jnp.zeros_like(acc)
        slots_out[...] = jnp.zeros_like(slots_out)

    def in_unit(j):
        low = sum(count for _, count in units[:j])
        return jnp.logical_and(i >= low, i < low + units[j][1])

    for j in range(u):

        @pl.when(in_unit(j))
        def _(j=j):
            x_scr[...] = xs[j][...]
            mix_scr[...] = mixes[j][...]
            for s in range(n):
                cot_scr[pl.ds(s * chunk, chunk), :] = cots[j][s][0]

    mods = mods_ref[pl.ds(i, 1), :]
    gate_one, shift_two, scale_two, gate_two = (
        mods[:, m * width : (m + 1) * width] for m in (2, 3, 4, 5)
    )
    mixed = mix_scr[...]
    branch = dot(mixed, mixer_w[...]) + mixer_b[...]
    middle = x_scr[...].astype(F32) + gate_one * branch
    normed, inverse = layer_norm(middle)
    normed_mid = (normed * (1.0 + scale_two) + shift_two).astype(BF16)
    hidden = dot(normed_mid, hidden_w[...]) + hidden_b[...]
    square = hidden * hidden
    bend = 0.7978845608028654 * 0.044715
    curve = jnp.tanh(hidden * (0.7978845608028654 + bend * square))
    half = 0.5 + 0.5 * curve
    active = (hidden * half).astype(BF16)
    slope = half + (0.5 * hidden) * (1.0 - curve * curve) * (0.7978845608028654 + 3.0 * bend * square)
    output = dot(active, output_w[...]) + output_b[...]
    cot = cot_scr[...].astype(F32)
    if valid_ref is not None:
        cot = cot * valid_ref[0]
    result = (middle + gate_two * output).astype(BF16)
    for j in range(u):

        @pl.when(in_unit(j))
        def _(j=j):
            for s in range(n):
                outs[j][s][0] = result[s * chunk : (s + 1) * chunk]

    output_grad = (gate_two * cot).astype(BF16)
    gate_two_grad = column_sum(cot * output)
    ow_acc[...] += dot(output_grad.T, active)
    ob_acc[...] += column_sum(output_grad.astype(F32))
    active_grad = dot_nt(output_grad, output_w[...])
    hidden_grad_wide = active_grad * slope
    hidden_grad = hidden_grad_wide.astype(BF16)
    hw_acc[...] += dot(normed_mid.T, hidden_grad)
    hb_acc[...] += column_sum(hidden_grad.astype(F32))
    mid_grad = dot_nt(hidden_grad, hidden_w[...])
    scale_two_grad = column_sum(mid_grad * normed)
    shift_two_grad = column_sum(mid_grad)
    middle_grad = cot + norm_back(mid_grad * (1.0 + scale_two), normed, inverse)
    middle_out[...] = middle_grad
    gate_one_grad = column_sum(middle_grad * branch)
    branch_grad = (gate_one * middle_grad).astype(BF16)
    mw_acc[...] += dot(mixed.T, branch_grad)
    mb_acc[...] += column_sum(branch_grad.astype(F32))
    mixed_grad_out[...] = dot_nt(branch_grad, mixer_w[...]).astype(BF16)
    slots_out[pl.ds(i, 1), :] = jnp.concatenate(
        [gate_one_grad, shift_two_grad, scale_two_grad, gate_two_grad], axis=1
    )

    @pl.when(i == total - 1)
    def _():
        ff = ow_acc.shape[1]
        grads_out[:ff, :] = ow_acc[...].T.astype(BF16)
        for j in range(ff // width):
            lo = ff + j * width
            grads_out[lo : lo + width, :] = hw_acc[:, j * width : (j + 1) * width].astype(BF16)
        grads_out[2 * ff : 2 * ff + width, :] = mw_acc[...].astype(BF16)
        rows = [ob_acc[...]]
        rows += [hb_acc[:, j * width : (j + 1) * width] for j in range(ff // width)]
        rows += [mb_acc[...], jnp.zeros((SMALL - 2 - ff // width, width), F32)]
        base = 2 * ff + width
        grads_out[base : base + SMALL, :] = jnp.concatenate(rows, axis=0).astype(BF16)
        rest = grads_out.shape[0] - base - SMALL
        grads_out[base + SMALL :, :] = jnp.zeros((rest, width), BF16)


def feed(units, n, chunk, valid, xs, mixes, cots, mods, weights, grad_rows):
    width, ff = weights[2].shape
    total = sum(count for _, count in units)
    shape = jax.ShapeDtypeStruct
    lows = [sum(count for _, count in units[:j]) for j in range(len(units))]

    def clip(j):
        return lambda i: jnp.clip(i - lows[j], 0, units[j][1] - 1)

    def rows_of(j):
        at = clip(j)
        return pl.BlockSpec((BLOCK, width), lambda i: (at(i), 0))

    def chunks_of(j):
        at = clip(j)
        return pl.BlockSpec((1, chunk, width), lambda i: (at(i), 0, 0))

    unit_ids = range(len(units))
    in_specs = [rows_of(j) for j in unit_ids] * 2
    in_specs += [chunks_of(j) for j in unit_ids for _ in range(n)]
    in_specs += [full(mods.shape)] + [full(w.shape) for w in weights]
    outs, out_specs = [], []
    for j in unit_ids:
        for _ in range(n):
            outs.append(shape((units[j][1], chunk, width), BF16))
            out_specs.append(chunks_of(j))
    outs += [shape((total * BLOCK, width), F32), shape((total * BLOCK, width), BF16)]
    out_specs += [pl.BlockSpec((BLOCK, width), lambda i: (i, 0))] * 2
    outs += [shape((grad_rows, width), BF16), shape((8, 4 * width), F32)]
    out_specs += [full((grad_rows, width)), full((8, 4 * width))]
    kernel = partial(feed_kernel, units, n, chunk, width)
    arrays = [*xs, *mixes, *[c for unit in cots for c in unit], mods, *weights]
    if valid is None:
        kernel = partial(kernel, None)
    else:
        in_specs, arrays = [SMEM] + in_specs, [valid] + arrays
    flops = total * BLOCK * 2 * (6 * width * ff + 3 * width * width)
    found = pl.pallas_call(
        kernel,
        grid=(total,),
        in_specs=in_specs,
        out_specs=out_specs,
        out_shape=outs,
        scratch_shapes=[
            pltpu.VMEM((BLOCK, width), BF16),
            pltpu.VMEM((BLOCK, width), BF16),
            pltpu.VMEM((BLOCK, width), BF16),
            pltpu.VMEM((width, ff), F32),
            pltpu.VMEM((width, ff), F32),
            pltpu.VMEM((width, width), F32),
            pltpu.VMEM((1, width), F32),
            pltpu.VMEM((1, ff), F32),
            pltpu.VMEM((1, width), F32),
        ],
        compiler_params=params(),
        cost_estimate=pl.CostEstimate(flops=flops, bytes_accessed=16 * MIB, transcendentals=0),
        name="feed",
    )(*arrays)
    pieces = [found[j * n : (j + 1) * n] for j in unit_ids]
    return pieces, found[len(units) * n :]


def finish_kernel(units, n, chunk, width, counts, *refs):
    u = len(units)
    xs, owns, refs = refs[:u], refs[u : 2 * u], refs[2 * u :]
    others = []
    for count in counts:
        others.append(refs[:count])
        refs = refs[count:]
    middle_ref, mods_ref, refs = refs[0], refs[1], refs[2:]
    outs, refs = [refs[i * n : (i + 1) * n] for i in range(u)], refs[u * n :]
    slots_out, x_scr, g_scr = refs
    i = pl.program_id(0)

    @pl.when(i == 0)
    def _():
        slots_out[...] = jnp.zeros_like(slots_out)

    def in_unit(j):
        low = sum(count for _, count in units[:j])
        return jnp.logical_and(i >= low, i < low + units[j][1])

    for j in range(u):

        @pl.when(in_unit(j))
        def _(j=j):
            x_scr[...] = xs[j][...]
            grad = owns[j][...]
            for other in others[j]:
                grad = grad + other[...].astype(F32)
            g_scr[...] = grad

    scale_one = mods_ref[pl.ds(i, 1), width : 2 * width]
    normed, inverse = layer_norm(x_scr[...].astype(F32))
    grad = g_scr[...]
    slots_out[pl.ds(i, 1), :] = jnp.concatenate(
        [column_sum(grad), column_sum(grad * normed)], axis=1
    )
    result = middle_ref[...] + norm_back(grad * (1.0 + scale_one), normed, inverse)
    result = result.astype(BF16)
    for j in range(u):

        @pl.when(in_unit(j))
        def _(j=j):
            for s in range(n):
                outs[j][s][0] = result[s * chunk : (s + 1) * chunk]


def finish(units, n, chunk, xs, owns, others, middle, mods):
    width = middle.shape[1]
    total = sum(count for _, count in units)
    shape = jax.ShapeDtypeStruct
    lows = [sum(count for _, count in units[:j]) for j in range(len(units))]

    def clip(j):
        return lambda i: jnp.clip(i - lows[j], 0, units[j][1] - 1)

    def rows_of(j):
        at = clip(j)
        return pl.BlockSpec((BLOCK, width), lambda i: (at(i), 0))

    def chunks_of(j):
        at = clip(j)
        return pl.BlockSpec((1, chunk, width), lambda i: (at(i), 0, 0))

    unit_ids = range(len(units))
    in_specs = [rows_of(j) for j in unit_ids] * 2
    in_specs += [rows_of(j) for j in unit_ids for _ in others[j]]
    in_specs += [pl.BlockSpec((BLOCK, width), lambda i: (i, 0)), full(mods.shape)]
    outs = [shape((units[j][1], chunk, width), BF16) for j in unit_ids for _ in range(n)]
    out_specs = [chunks_of(j) for j in unit_ids for _ in range(n)]
    found = pl.pallas_call(
        partial(finish_kernel, units, n, chunk, width, [len(o) for o in others]),
        grid=(total,),
        in_specs=in_specs,
        out_specs=out_specs + [full((8, 2 * width))],
        out_shape=outs + [shape((8, 2 * width), F32)],
        scratch_shapes=[pltpu.VMEM((BLOCK, width), BF16), pltpu.VMEM((BLOCK, width), F32)],
        compiler_params=params(),
        cost_estimate=pl.CostEstimate(
            flops=total * BLOCK * width * 40, bytes_accessed=total * BLOCK * width * 12, transcendentals=0
        ),
        name="finish",
    )(*xs, *owns, *[o for unit in others for o in unit], middle, mods)
    return [found[j * n : (j + 1) * n] for j in unit_ids], found[-1]


def xor_permute(value, mask, size):
    return lax.ppermute(value, ("rows", "band"), [(i, i ^ mask) for i in range(size)])


def stages_of(rows, bands):
    band_bits = bands.bit_length() - 1
    bits = (rows * bands).bit_length() - 1
    core = band_bits
    rest = [b for b in range(bits) if b != core and b >= core] + [0]
    rest += [b for b in range(1, core)]
    return [[core]] + [rest[i : i + 2] for i in range(0, len(rest), 2)]


def digit_of(me, stage):
    return sum(((me >> b) & 1) << i for i, b in enumerate(stage))


def mask_of(t, stage):
    return sum(((t >> i) & 1) << b for i, b in enumerate(stage))


def reduce_scatter(value, me, stages, size):
    for stage in stages:
        parts = 1 << len(stage)
        rows = value.shape[0] // parts
        digit = digit_of(me, stage)
        received = [
            xor_permute(
                lax.dynamic_slice_in_dim(value, (digit ^ t) * rows, rows, 0), mask_of(t, stage), size
            )
            for t in range(1, parts)
        ]
        mine = lax.dynamic_slice_in_dim(value, digit * rows, rows, 0).astype(F32)
        for part in received:
            mine = mine + part.astype(F32)
        value = mine.astype(BF16)
    return value


def gather_all(value, me, stages, size):
    for stage in reversed(stages):
        parts = 1 << len(stage)
        rows = value.shape[0]
        digit = digit_of(me, stage)
        whole = jnp.zeros((rows * parts,) + value.shape[1:], value.dtype)
        for t in range(parts):
            part = value if t == 0 else xor_permute(value, mask_of(t, stage), size)
            whole = lax.dynamic_update_slice_in_dim(whole, part, (digit ^ t) * rows, 0)
        value = whole
    return value


def body(
    patches,
    condition_table,
    condition_index,
    image_lengths,
    modulate_weight,
    modulate_bias,
    triple_weight,
    query_bias,
    value_bias,
    mixer_weight,
    mixer_bias,
    hidden_weight,
    hidden_bias,
    output_weight,
    output_bias,
    cotangent,
):
    band = lax.axis_index("band")
    n = lax.axis_size("band")
    size = n * lax.axis_size("rows")
    everyone = lax.axis_index(("rows", "band"))
    rows, band_length, width = patches.shape
    ff = hidden_weight.shape[1]
    length = band_length * n
    big = length // 2
    chunk = band_length // (2 * HALF)
    assert length == 2 * HALF * BLOCK
    plan = Plan(rows, n)
    units = plan.units()
    me = band.astype(jnp.int32).reshape(1)
    stages = stages_of(size // n, n)

    def deal(pieces):
        return [
            piece if i % n == 0 else xor_permute(piece, i % n, size) for i, piece in enumerate(pieces)
        ]

    def by_unit(pieces):
        return [pieces[j * n : (j + 1) * n] for j in range(len(units))]

    x_pieces = by_unit(deal(pack(plan, chunk, big, me, image_lengths, patches)))

    is_big = (image_lengths == big).astype(jnp.int32)
    big_count = jnp.sum(is_big, axis=1)
    lead = jnp.sum((jnp.cumsum(is_big, axis=1) == 0).astype(jnp.int32), axis=1)
    start = jnp.where(big_count == 1, lead, 0)
    flags, half_rows, places = [], [], []
    for name, count in units:
        half_row = jnp.minimum(plan.half_row(name, band), plan.halves - 1)
        for t in range(HALF // count):
            first = 0 if name == "whole" else ((band % plan.group) ^ t) * count
            half_rows += [half_row] * count
            places += [first + k for k in range(count)]
        of_row, half = big_count[half_row // 2], half_row % 2
        flags.append(((of_row == 2) | ((of_row == 1) & (half == 0))).astype(jnp.int32).reshape(1))
    half_rows, places = jnp.stack(half_rows), jnp.stack([jnp.asarray(p, jnp.int32) for p in places])
    row_ids, half_ids = half_rows // 2, half_rows % 2
    bigs, starts = big_count[row_ids], start[row_ids]
    single = jnp.where(half_ids == 0, starts, jnp.where(places < starts, places, places + 1))
    slot = jnp.where(bigs == 2, half_ids, jnp.where(bigs == 0, HALF * half_ids + places, single))
    index = condition_index[row_ids, slot]
    choose = (index[:, None] == jnp.arange(condition_table.shape[0], dtype=jnp.int32)).astype(BF16)
    activity = jax.nn.silu(dot(choose, condition_table)).astype(BF16)
    mods = dot(activity, modulate_weight) + modulate_bias.astype(F32)

    wide = lambda v: v.astype(F32).reshape(1, -1)
    attended, xs, mixes = [], [], []
    for j, (name, count) in enumerate(units):
        lo = j * HALF
        others = []
        if count < HALF:
            own = jnp.stack(x_pieces[j], axis=1).reshape(count * BLOCK, width)
            others = [xor_permute(own, t, size) for t in range(1, HALF // count)]
        found = attend(
            n,
            count,
            HALF,
            chunk,
            flags[j],
            x_pieces[j],
            others,
            mods[lo : lo + HALF],
            triple_weight,
            wide(query_bias),
            wide(value_bias),
        )
        xs.append(found[0])
        attended.append(found[1:8])
        mixes.append(found[8])

    if len(units) == 2:
        own_rows = [*range(HALF), *range(HALF, HALF + units[1][1])]
    else:
        own_rows = [*range(units[0][1])]
    total = len(own_rows)
    own_mods = jnp.pad(mods[:total], ((0, 8 - total), (0, 0)))
    valid = None
    if plan.idle:
        valid = (plan.half_row("shared", band) < plan.halves).astype(F32).reshape(1)

    tied = lax.optimization_barrier((cotangent, x_pieces[-1][-1]))
    c_pieces = by_unit(deal(pack(plan, chunk, big, me, image_lengths, tied[0])))

    grad_rows = 2 * ff + width + 128
    weights = [
        mixer_weight,
        wide(mixer_bias),
        hidden_weight,
        wide(hidden_bias),
        output_weight,
        wide(output_bias),
    ]
    out_pieces, (middle_grad, mixed_grad, feed_grads, feed_slots) = feed(
        units, n, chunk, valid, xs, mixes, c_pieces, own_mods, weights, grad_rows
    )
    out_back = [p for unit in out_pieces for p in deal(unit)]
    block_out = unpack(plan, chunk, big, me, image_lengths, out_back, BF16)
    feed_part = reduce_scatter(feed_grads, everyone, stages, size)

    owns, others, triple_grads, triple_sums = [], [], [], []
    lows = [0, HALF] if len(units) == 2 else [0]
    results = {}
    for j in reversed(range(len(units))):
        count = units[j][1]
        grad = mixed_grad[lows[j] * BLOCK : (lows[j] + count) * BLOCK]
        results[j] = attend_back(count, HALF, flags[j], attended[j], grad, triple_weight)
    for j in range(len(units)):
        found = results[j]
        owns.append(found[0])
        others.append([xor_permute(o, t + 1, size) for t, o in enumerate(found[1:-2])])
        triple_grads.append(found[-2])
        triple_sums.append(found[-1])
    triple_grad = sum(triple_grads)
    triple_sum = sum(triple_sums)[:1]
    triple_rows = jnp.concatenate(
        [triple_grad[:, m * width : (m + 1) * width] for m in range(3)]
        + [triple_sum[:, :width], triple_sum[:, 2 * width :], jnp.zeros((126, width), F32)],
        axis=0,
    ).astype(BF16)
    extra = -triple_rows.shape[0] % size
    if extra:
        triple_rows = jnp.pad(triple_rows, ((0, extra), (0, 0)))
    triple_part = reduce_scatter(triple_rows, everyone, stages, size)

    grad_pieces, finish_slots = finish(units, n, chunk, xs, owns, others, middle_grad, own_mods)
    grad_back = [p for unit in grad_pieces for p in deal(unit)]
    patch_grad = unpack(plan, chunk, big, me, image_lengths, grad_back, F32)

    slots = jnp.concatenate([finish_slots[:total], feed_slots[:total]], axis=1).astype(BF16)
    slots = gather_all(jnp.concatenate([slots, activity[:total]], axis=1), everyone, stages, size)
    slot_grads, activities = slots[:, : 6 * width], slots[:, 6 * width :]
    modulate_w_grad = lax.dot_general(
        activities, slot_grads, (((0,), (0,)), ((), ())), preferred_element_type=F32
    )
    modulate_b_grad = jnp.sum(slot_grads.astype(F32), axis=0)

    feed_all = gather_all(feed_part, everyone, stages, size).astype(F32)
    triple_all = gather_all(triple_part, everyone, stages, size).astype(F32)
    base = 2 * ff + width
    hidden_w_grad = jnp.concatenate(
        [feed_all[ff + j * width : ff + (j + 1) * width] for j in range(ff // width)], axis=1
    )
    triple_w_grad = jnp.concatenate(
        [triple_all[m * width : (m + 1) * width] for m in range(3)], axis=1
    )
    return (
        block_out,
        patch_grad,
        modulate_w_grad,
        modulate_b_grad,
        triple_w_grad,
        triple_all[3 * width],
        triple_all[3 * width + 1],
        feed_all[2 * ff : base],
        feed_all[base + 1 + ff // width],
        hidden_w_grad,
        feed_all[base + 1 : base + 1 + ff // width].reshape(-1),
        feed_all[:ff],
        feed_all[base],
    )


def solution(mesh):
    return jax.shard_map(
        body,
        mesh=mesh,
        in_specs=(
            P("rows", None, "band"),
            P(),
            P("rows", None),
            P("rows", None),
            P(),
            P(),
            P(),
            P(),
            P(),
            P(),
            P(),
            P(),
            P(),
            P(),
            P(),
            P("rows", None, "band"),
        ),
        out_specs=(
            P("rows", None, "band"),
            P("rows", None, "band"),
            P(),
            P(),
            P(),
            P(),
            P(),
            P(),
            P(),
            P(),
            P(),
            P(),
            P(),
        ),
        check_vma=False,
    )
```

```python
from functools import partial

import jax
import jax.numpy as jnp
from jax import lax
from jax.experimental import pallas as pl
from jax.experimental.pallas import tpu as pltpu
from jax.sharding import PartitionSpec as P

HEADS = 6
HEAD_DIM = 64
PAIRS = HEADS // 2
LANES = 128
BLOCK = 256
HALF = 4
EPSILON = 1e-06
ONES = 16
TIE = 8
F32 = jnp.float32
BF16 = jnp.bfloat16
MIB = 1 << 20


def dot(left, right):
    return jnp.dot(left, right, preferred_element_type=F32)


def dot_nt(left, right):
    return lax.dot_general(left, right, (((1,), (1,)), ((), ())), preferred_element_type=F32)


def params(limit=56, **more):
    return pltpu.CompilerParams(vmem_limit_bytes=limit * MIB, **more)


def cost(micros):
    return pl.CostEstimate(flops=0, bytes_accessed=int(micros * 3e6), transcendentals=0)


def full(shape):
    return pl.BlockSpec(shape, lambda *_: (0,) * len(shape))


SMEM = pl.BlockSpec(memory_space=pltpu.SMEM)


def row_layout(lens_ref, row, slots, big):
    count = jnp.int32(0)
    before = jnp.int32(0)
    for j in range(slots):
        is_big = (lens_ref[row, j] == big).astype(jnp.int32)
        before = before + jnp.where(count + is_big == 0, 1, 0)
        count = count + is_big
    return count, jnp.where(count == 1, before, 0)


def chunk_of(start, half, k):
    return jnp.where(half == 0, start + k, jnp.where(k < start, k, k + HALF))


class Plan:
    def __init__(self, rows, bands):
        self.rows, self.bands = rows, bands
        self.halves = 2 * rows
        self.whole = self.halves // bands
        assert self.whole <= 1
        self.rest = self.halves - self.whole * bands
        self.group = 1
        while self.rest and self.rest * self.group * 2 <= bands and self.group < HALF:
            self.group *= 2
        self.idle = self.rest * self.group != bands
        self.own = HALF // self.group

    @property
    def total(self):
        return sum(count for _, count in self.units())

    def units(self):
        found = []
        if self.whole:
            found.append(("whole", HALF))
        if self.rest:
            found.append(("shared", self.own))
        return found

    def half_row(self, name, device):
        if name == "whole":
            return device
        return self.whole * self.bands + device // self.group

    def first(self, name, device):
        return 0 if name == "whole" else (device % self.group) * self.own


def pack_kernel(plan, chunk, slots, big, apart, me_ref, lens_ref, x_ref, *outs):
    for s in range(plan.bands):
        dest = me_ref[0] ^ s if apart else s
        at = 0
        for name, count in plan.units():
            half_row = jnp.minimum(plan.half_row(name, dest), plan.halves - 1)
            row, half = half_row // 2, half_row % 2
            start = row_layout(lens_ref, row, slots, big)[1]
            for k in range(count):
                source = chunk_of(start, half, plan.first(name, dest) + k)
                rows = pl.ds(pl.multiple_of(source * chunk, chunk), chunk)
                if apart:
                    outs[s][at] = x_ref[row, rows, :]
                else:
                    outs[0][dest, at] = x_ref[row, rows, :]
                at += 1


def pack(plan, chunk, big, me, lens, x, apart):
    shape = (plan.total, chunk, x.shape[2])
    shapes = [shape] * plan.bands if apart else [(plan.bands,) + shape]
    found = pl.pallas_call(
        partial(pack_kernel, plan, chunk, lens.shape[1], big, apart),
        in_specs=[SMEM, SMEM, full(x.shape)],
        out_specs=[full(s) for s in shapes],
        out_shape=[jax.ShapeDtypeStruct(s, x.dtype) for s in shapes],
        grid=(1,),
        compiler_params=params(32),
        cost_estimate=cost(0.1),
        name="pack",
    )(me, lens, x)
    return found if apart else found[0]


def unpack_kernel(plan, chunk, slots, big, lens_ref, piece_ref, out_ref):
    for owner in range(plan.bands):
        at = 0
        for name, count in plan.units():
            half_row = plan.half_row(name, owner)
            if half_row < plan.halves:
                row, half = half_row // 2, half_row % 2
                start = row_layout(lens_ref, row, slots, big)[1]
                for k in range(count):
                    source = chunk_of(start, half, plan.first(name, owner) + k)
                    rows = pl.ds(pl.multiple_of(source * chunk, chunk), chunk)
                    out_ref[row, rows, :] = piece_ref[owner, at + k].astype(out_ref.dtype)
            at += count


def unpack(plan, chunk, big, lens, pieces, dtype):
    shape = (plan.rows, chunk * 2 * HALF, pieces.shape[3])
    return pl.pallas_call(
        partial(unpack_kernel, plan, chunk, lens.shape[1], big),
        in_specs=[SMEM, full(pieces.shape)],
        out_specs=full(shape),
        out_shape=jax.ShapeDtypeStruct(shape, dtype),
        grid=(1,),
        compiler_params=params(32),
        cost_estimate=cost(0.1),
        name="unpack",
    )(lens, pieces)


def collect_kernel(n, low, count, chunk, me_ref, *refs):
    for b in range(count):
        for s in range(n):
            at = pl.multiple_of(b * BLOCK + (me_ref[0] ^ s) * chunk, chunk)
            refs[n][pl.ds(at, chunk), :] = refs[s][low + b]


def collect(n, low, count, chunk, me, pieces):
    width = pieces[0].shape[2]
    return pl.pallas_call(
        partial(collect_kernel, n, low, count, chunk),
        in_specs=[SMEM] + [full(p.shape) for p in pieces],
        out_specs=full((count * BLOCK, width)),
        out_shape=jax.ShapeDtypeStruct((count * BLOCK, width), BF16),
        grid=(1,),
        compiler_params=params(16),
        cost_estimate=cost(0.1),
        name="collect",
    )(me, *pieces)


def prepare_kernel(plan, slots, big, me_ref, lens_ref, index_ref, table_ref, weight_ref, bias_ref, *refs):
    mods_out, activity_out, flags_out, table_scr, activity_scr = refs
    table_scr[...] = table_ref[...].astype(F32)
    activity_scr[...] = jnp.zeros_like(activity_scr)
    at = 0
    for j, (name, count) in enumerate(plan.units()):
        half_row = jnp.minimum(plan.half_row(name, me_ref[0]), plan.halves - 1)
        row, half = half_row // 2, half_row % 2
        bigs, start = row_layout(lens_ref, row, slots, big)
        is_big = jnp.logical_or(bigs == 2, jnp.logical_and(bigs == 1, half == 0))
        flags_out[j] = is_big.astype(jnp.int32)
        for t in range(HALF // count):
            first = 0 if count == HALF else ((me_ref[0] % plan.group) ^ t) * count
            for k in range(count):
                place = first + k
                single = jnp.where(half == 0, start, jnp.where(place < start, place, place + 1))
                slot = jnp.where(bigs == 2, half, jnp.where(bigs == 0, HALF * half + place, single))
                chosen = table_scr[pl.ds(index_ref[row, slot], 1), :]
                activity_scr[at : at + 1, :] = chosen * (1.0 / (1.0 + jnp.exp(-chosen)))
                at += 1
    activity = activity_scr[...].astype(BF16)
    activity_out[...] = activity.astype(F32)
    mods_out[...] = dot(activity, weight_ref[...]) + as_row(bias_ref)


def prepare(plan, big, me, lens, index, table, weight, bias):
    width = table.shape[1]
    shape = jax.ShapeDtypeStruct
    arrays = [table, weight, bias]
    return pl.pallas_call(
        partial(prepare_kernel, plan, lens.shape[1], big),
        in_specs=[SMEM] * 3 + [full(a.shape) for a in arrays],
        out_specs=[full((8, weight.shape[1])), full((8, width)), SMEM],
        out_shape=[
            shape((8, weight.shape[1]), F32),
            shape((8, width), F32),
            shape((2,), jnp.int32),
        ],
        grid=(1,),
        scratch_shapes=[pltpu.VMEM(table.shape, F32), pltpu.VMEM((8, width), F32)],
        compiler_params=params(32),
        cost_estimate=cost(0.1),
        name="prepare",
    )(me, lens, index, *arrays)


def layer_norm(values):
    centre = values - jnp.mean(values, axis=-1, keepdims=True)
    inverse = lax.rsqrt(jnp.mean(centre * centre, axis=-1, keepdims=True) + EPSILON)
    return centre * inverse, inverse


def norm_back(grad, normed, inverse):
    return inverse * (
        grad
        - jnp.mean(grad, axis=-1, keepdims=True)
        - normed * jnp.mean(grad * normed, axis=-1, keepdims=True)
    )


def as_row(ref):
    return ref[...].astype(F32).reshape(1, -1)


def column_sum(values):
    return jnp.sum(values, axis=0, keepdims=True)


def attend_kernel(n, unit, low, nq, nk, chunk, width, me_ref, flag_ref, *refs):
    pieces, refs = refs[:n], refs[n:]
    count = nk // nq - 1
    others, refs = refs[:count], refs[count:]
    mods_ref, weight_ref, query_bias_ref, value_bias_ref = refs[:4]
    x_out, hint_out, q_out, k_out, v_out, e_out, ot_out, inv_out, mixed_out = refs[4:13]
    k_scr, qt_scr, vt_scr = refs[13:]
    p = pl.program_id(0)

    @pl.when(p == 0)
    def _():
        qt_scr[...] = jnp.zeros_like(qt_scr)
        for h in range(HEADS):
            vt_scr[h, HEAD_DIM:, :] = jnp.ones((ONES, nk * BLOCK), BF16)
        for b in range(nk):
            rows = pl.ds(b * BLOCK, BLOCK)
            if b < nq:
                for s in range(n):
                    at = pl.multiple_of(b * BLOCK + (me_ref[0] ^ s) * chunk, chunk)
                    x_out[pl.ds(at, chunk), :] = pieces[s][low + b]
            else:
                t, inner = b // nq - 1, b % nq
                x_out[rows, :] = others[t][pl.ds(inner * BLOCK, BLOCK), :]
            source = x_out[rows, :].astype(F32)
            normed = layer_norm(source)[0]
            shift = mods_ref[low + b : low + b + 1, 0:width]
            scale = mods_ref[low + b : low + b + 1, width : 2 * width]
            hin = (normed * (1.0 + scale) + shift).astype(BF16)
            hint_out[:, rows] = hin.T
            triple = dot(hin, weight_ref[...])
            keys = triple[:, width : 2 * width].astype(BF16)
            values = (triple[:, 2 * width :] + as_row(value_bias_ref)).astype(BF16)
            values_t = values.T
            for j in range(PAIRS):
                lanes = slice(j * LANES, (j + 1) * LANES)
                k_scr[j, rows, :] = keys[:, lanes]
                k_out[j, rows, :] = keys[:, lanes]
                v_out[j, rows, :] = values[:, lanes]
            for h in range(HEADS):
                vt_scr[h, :HEAD_DIM, rows] = values_t[h * HEAD_DIM : (h + 1) * HEAD_DIM]
            if b < nq:
                query = (triple[:, :width] + as_row(query_bias_ref)) * (HEAD_DIM**-0.5)
                query = query.astype(BF16)
                for j in range(PAIRS):
                    q_out[j, rows, :] = query[:, j * LANES : (j + 1) * LANES]
                query_t = query.T
                for h in range(HEADS):
                    to = (h % 2) * HEAD_DIM
                    qt_scr[h, to : to + HEAD_DIM, rows] = query_t[
                        h * HEAD_DIM : (h + 1) * HEAD_DIM
                    ]

    def tile(columns, krows):
        found = []
        for hh in range(2):
            h = 2 * p + hh
            scores = dot(k_scr[p, krows, :], qt_scr[h, :, columns])
            exps = jnp.exp(scores - jnp.max(scores, axis=0, keepdims=True)).astype(BF16)
            e_out[hh, krows, columns] = exps
            summed = dot(vt_scr[h, :, krows], exps)
            inverse = 1.0 / summed[HEAD_DIM : HEAD_DIM + 1]
            found.append(summed[:HEAD_DIM] * inverse)
            inv_out[0, hh : hh + 1, columns] = inverse
        both = jnp.concatenate(found, axis=0)
        ot_out[0, :, columns] = both
        mixed_out[columns, :] = both.T.astype(BF16)

    @pl.when(flag_ref[unit] == 1)
    def _():
        tile(pl.ds(0, nq * BLOCK), pl.ds(0, nk * BLOCK))

    @pl.when(flag_ref[unit] == 0)
    def _():
        for b in range(nq):
            tile(pl.ds(b * BLOCK, BLOCK), pl.ds(b * BLOCK, BLOCK))


def attend(n, unit, low, nq, nk, chunk, me, flag, pieces, others, mods, weight, query_bias, value_bias):
    width = weight.shape[0]
    qs, ks = nq * BLOCK, nk * BLOCK
    shape = jax.ShapeDtypeStruct
    outs = [
        (shape((ks, width), BF16), None),
        (shape((width, ks), BF16), None),
        (shape((PAIRS, qs, LANES), BF16), None),
        (shape((PAIRS, ks, LANES), BF16), None),
        (shape((PAIRS, ks, LANES), BF16), None),
        (shape((HEADS, ks, qs), BF16), pl.BlockSpec((2, ks, qs), lambda p: (p, 0, 0))),
        (shape((PAIRS, LANES, qs), F32), pl.BlockSpec((1, LANES, qs), lambda p: (p, 0, 0))),
        (shape((PAIRS, 8, qs), F32), pl.BlockSpec((1, 8, qs), lambda p: (p, 0, 0))),
        (shape((qs, width), BF16), pl.BlockSpec((qs, LANES), lambda p: (0, p))),
    ]
    arrays = [*pieces, *others, mods, weight, query_bias, value_bias]
    flops = 2 * ks * width * 3 * width + 4 * HEADS * qs * ks * HEAD_DIM * 4
    return pl.pallas_call(
        partial(attend_kernel, n, unit, low, nq, nk, chunk, width),
        grid=(PAIRS,),
        in_specs=[SMEM, SMEM] + [full(a.shape) for a in arrays],
        out_specs=[spec or full(s.shape) for s, spec in outs],
        out_shape=[s for s, _ in outs],
        scratch_shapes=[
            pltpu.VMEM((PAIRS, ks, LANES), BF16),
            pltpu.VMEM((HEADS, LANES, qs), BF16),
            pltpu.VMEM((HEADS, HEAD_DIM + ONES, ks), BF16),
        ],
        compiler_params=params(),
        cost_estimate=cost(0.1),
        name="attend",
    )(me, flag, *arrays)


def back_tile(qlow, qsize, klow, ksize, e_ref, q_ref, k_ref, v_ref, ot_ref, inv_ref, grad_ref):
    columns, krows = pl.ds(qlow, qsize), pl.ds(klow, ksize)
    lane = lax.broadcasted_iota(jnp.int32, (qsize, LANES), 1)
    grad_t = grad_ref[columns, :].astype(F32).T
    keys_t = k_ref[0, krows, :].T
    query = q_ref[0, columns, :]
    zeros = jnp.zeros((HEAD_DIM, qsize), BF16)
    found, keys_grad, values_grad = [], None, None
    for hh in range(2):
        part = slice(hh * HEAD_DIM, (hh + 1) * HEAD_DIM)
        scaled = (grad_t[part] * inv_ref[0, hh : hh + 1, columns]).astype(BF16)
        delta = column_sum(scaled.astype(F32) * ot_ref[0, part, columns])
        masked = jnp.concatenate([scaled, zeros] if hh == 0 else [zeros, scaled], axis=0)
        exps = e_ref[hh, krows, columns]
        prob_grad = dot(v_ref[0, krows, :], masked)
        score_grad = (exps.astype(F32) * (prob_grad - delta)).astype(BF16)
        own = (lane < HEAD_DIM) if hh == 0 else (lane >= HEAD_DIM)
        values_part = dot_nt(exps, masked)
        keys_part = dot(score_grad, jnp.where(own, query, jnp.zeros_like(query)))
        values_grad = values_part if hh == 0 else values_grad + values_part
        keys_grad = keys_part if hh == 0 else keys_grad + keys_part
        found.append(dot(keys_t[part], score_grad))
    both = jnp.concatenate(found, axis=0) * (HEAD_DIM**-0.5)
    return both.T.astype(BF16), keys_grad.astype(BF16), values_grad.astype(BF16)


def shared_back_kernel(nq, nk, flag_ref, *refs):
    tile_refs, (hint_ref, weight_ref, own_out), refs = refs[:7], refs[7:10], refs[10:]
    others_out, (tw_out, tb_out, tg_scr) = refs[:-3], refs[-3:]
    p = pl.program_id(0)
    qs, rest = nq * BLOCK, (nk - nq) * BLOCK

    def tile(qlow, qsize, klow, ksize):
        query_grad, keys_grad, values_grad = back_tile(qlow, qsize, klow, ksize, *tile_refs)
        tg_scr[p, pl.ds(qlow, qsize), :] = query_grad
        tg_scr[PAIRS + p, pl.ds(klow, ksize), :] = keys_grad
        tg_scr[2 * PAIRS + p, pl.ds(klow, ksize), :] = values_grad

    tg_scr[p, qs:, :] = jnp.zeros((rest, LANES), BF16)

    @pl.when(flag_ref[1] == 1)
    def _():
        tile(0, qs, 0, nk * BLOCK)

    @pl.when(flag_ref[1] == 0)
    def _():
        for j in (1, 2):
            tg_scr[j * PAIRS + p, qs:, :] = jnp.zeros((rest, LANES), BF16)
        for b in range(nq):
            tile(b * BLOCK, BLOCK, b * BLOCK, BLOCK)

    @pl.when(p == PAIRS - 1)
    def _():
        grads = jnp.concatenate([tg_scr[j] for j in range(3 * PAIRS)], axis=1)
        back = dot_nt(grads, weight_ref[...])
        own_out[...] = back[:qs]
        for t, out in enumerate(others_out):
            out[...] = back[(t + 1) * qs : (t + 2) * qs].astype(BF16)
        weight_grad = dot(hint_ref[...], grads)
        sums = column_sum(grads.astype(F32))
        for j in range(PAIRS):
            for m in range(3):
                low = (m * PAIRS + j) * LANES
                tw_out[j, :, m * LANES : (m + 1) * LANES] = weight_grad[:, low : low + LANES]
                tb_out[j, :, m * LANES : (m + 1) * LANES] = jnp.broadcast_to(
                    sums[:, low : low + LANES], (8, LANES)
                )


def whole_back_kernel(size, begun, last, flag_ref, *refs):
    tile_refs, hint_ref, refs = refs[:7], refs[7], refs[8:]
    if begun:
        tw_ref, tb_ref, refs = refs[0], refs[1], refs[2:]
    if last:
        me_ref, mixer_ref, earlier, refs = refs[0], refs[1], refs[2 : 1 + PAIRS], refs[1 + PAIRS :]
    tq_out, tk_out, tv_out, tb_out, refs = *refs[:4], refs[4:]

    def tile(qlow, qsize, klow, ksize):
        query_grad, keys_grad, values_grad = back_tile(qlow, qsize, klow, ksize, *tile_refs)
        tq_out[pl.ds(qlow, qsize), :] = query_grad
        tk_out[pl.ds(klow, ksize), :] = keys_grad
        tv_out[pl.ds(klow, ksize), :] = values_grad

    @pl.when(flag_ref[0] == 1)
    def _():
        tile(0, HALF * BLOCK, 0, HALF * BLOCK)

    @pl.when(flag_ref[0] == 0)
    def _():
        for b in range(HALF):
            tile(b * BLOCK, BLOCK, b * BLOCK, BLOCK)

    grads = jnp.concatenate([tq_out[...], tk_out[...], tv_out[...]], axis=1)
    weight_grad = dot(hint_ref[...], grads)
    sums = column_sum(grads.astype(F32))
    if begun:
        weight_grad, sums = weight_grad + tw_ref[0], sums + tb_ref[0, 0:1]
    tb_out[...] = jnp.broadcast_to(sums, tb_out.shape)
    if not last:
        refs[0][...] = weight_grad
        return
    first_out, second_out, rows_scr = refs
    width = weight_grad.shape[0]
    for m in range(3):
        lanes = slice(m * LANES, (m + 1) * LANES)
        rows = slice(m * width, (m + 1) * width)
        for j, ref in enumerate(earlier):
            rows_scr[rows, j * LANES : (j + 1) * LANES] = ref[:, lanes].astype(BF16)
        rows_scr[rows, (PAIRS - 1) * LANES :] = weight_grad[:, lanes].astype(BF16)
    rows_scr[3 * width : 4 * width, :] = mixer_ref[...].astype(BF16)
    if rows_scr.shape[0] > 4 * width:
        rows_scr[4 * width :, :] = jnp.zeros((rows_scr.shape[0] - 4 * width, width), BF16)
    spread_out(me_ref, rows_scr.shape[0] // size, size, rows_scr, (first_out, second_out))


def back_inputs(nq, nk, first, flag, kept, grad, low):
    hint, q, k, v, e, ot, inv = kept
    qs, ks = nq * BLOCK, nk * BLOCK
    by_pair = lambda *tail: pl.BlockSpec((1,) + tail, lambda p: (first + p, 0, 0))
    in_specs = [
        SMEM,
        pl.BlockSpec((2, ks, qs), lambda p: (first + p, 0, 0)),
        by_pair(qs, LANES),
        by_pair(ks, LANES),
        by_pair(ks, LANES),
        by_pair(LANES, qs),
        by_pair(8, qs),
        pl.BlockSpec((qs, LANES), lambda p: (low * BLOCK // qs, first + p)),
        full(hint.shape),
    ]
    return in_specs, [flag, e, q, k, v, ot, inv, grad, hint]


def back_cost(qs, ks, steps):
    flops = 8 * 2 * steps * qs * ks * HEAD_DIM * 4
    return pl.CostEstimate(flops=flops, bytes_accessed=4 * steps * qs * ks, transcendentals=0)


def shared_back(nq, nk, flag, kept, grad, low, weight):
    width = weight.shape[0]
    qs, ks = nq * BLOCK, nk * BLOCK
    in_specs, arrays = back_inputs(nq, nk, 0, flag, kept, grad, low)
    shape = jax.ShapeDtypeStruct
    outs = [shape((qs, width), F32)] + [shape((qs, width), BF16)] * (nk // nq - 1)
    outs += [shape((PAIRS, width, 3 * LANES), F32), shape((PAIRS, 8, 3 * LANES), F32)]
    return pl.pallas_call(
        partial(shared_back_kernel, nq, nk),
        grid=(PAIRS,),
        in_specs=in_specs + [full(weight.shape)],
        out_specs=[full(o.shape) for o in outs],
        out_shape=outs,
        scratch_shapes=[pltpu.VMEM((3 * PAIRS, ks, LANES), BF16)],
        compiler_params=params(),
        cost_estimate=cost(0.1),
        name="shared_back",
    )(*arrays, weight)


def whole_back(size, me, pair, flag, kept, grad, begun, mixer, earlier):
    width = mixer.shape[0]
    rows = HALF * BLOCK
    in_specs, arrays = back_inputs(HALF, HALF, pair, flag, kept, grad, 0)
    shape = jax.ShapeDtypeStruct
    if begun:
        in_specs += [pl.BlockSpec((1,) + b.shape[1:], lambda p: (pair, 0, 0)) for b in begun]
        arrays += begun
    outs = [shape((rows, LANES), BF16)] * 3 + [shape((8, 3 * LANES), F32)]
    last = pair == PAIRS - 1
    scratch = []
    if last:
        in_specs += [SMEM] + [full(a.shape) for a in (mixer, *earlier)]
        arrays += [me, mixer, *earlier]
        total = padded(4 * width, size)
        outs += [shape((total // 2, width), BF16)] * 2
        scratch = [pltpu.VMEM((total, width), BF16)]
    else:
        outs += [shape((width, 3 * LANES), F32)]
    return pl.pallas_call(
        partial(whole_back_kernel, size, bool(begun), last),
        grid=(1,),
        in_specs=in_specs,
        out_specs=[full(o.shape) for o in outs],
        out_shape=outs,
        scratch_shapes=scratch,
        compiler_params=params(),
        cost_estimate=cost(0.1),
        name="whole_back",
    )(*arrays)


def spread_out(me_ref, chunk, size, source, outs):
    half = size // 2
    for j, out in enumerate(outs):

        @pl.loop(0, half)
        def _(p, j=j, out=out):
            at = pl.multiple_of(((p + j * half) ^ me_ref[0]) * chunk, chunk)
            out[pl.ds(pl.multiple_of(p * chunk, chunk), chunk), :] = source[pl.ds(at, chunk), :]


def padded(rows, size):
    return rows + -rows % (16 * size)


STEP = 6
SPLIT = 1


def feed_kernel(units, n, chunk, width, size, masked, me_ref, *refs):
    total = sum(count for _, count in units)
    u = len(units)
    if masked:
        valid_ref, refs = refs[0], refs[1:]
    xs, mixes, cot_ref, refs = refs[:u], refs[u : 2 * u], refs[2 * u], refs[2 * u + 1 :]
    mods_ref, activity_ref, mixer_w, mixer_b, hidden_w, hidden_b, output_w, output_b = refs[:8]
    out_ref, refs = refs[8], refs[9:]
    middle_out, mixed_grad_out, first_out, second_out, mixer_out, small_out, refs = *refs[:6], refs[6:]
    middle_scr, branch_scr, out_acc, mid_acc, normed_scr, grad_scr, normed_t, grad_t = refs[:8]
    ow_acc, hw_acc, mw_acc, ob_acc, hb_acc, mb_acc, rows_scr, slots_acc = refs[8:]
    f = pl.program_id(0)
    part = ow_acc.shape[1] // SPLIT
    cut = lambda at: slice(at * width, (at + 1) * width)
    lows = [sum(count for _, count in units[:j]) for j in range(u)]

    def cotangent(b):
        cot = jnp.concatenate([cot_ref[s, b] for s in range(n)], axis=0).astype(F32)
        return cot * valid_ref[0] if masked else cot

    @pl.when(f == 0)
    def _():
        for acc in (out_acc, mid_acc, ow_acc, hw_acc, mw_acc, ob_acc, hb_acc, mb_acc, slots_acc):
            acc[...] = jnp.zeros_like(acc)
        for j in range(u):

            for b in range(units[j][1]):
                source = pl.ds(b * BLOCK, BLOCK)
                at = b + lows[j]
                rows = pl.ds(at * BLOCK, BLOCK)
                mods = mods_ref[at : at + 1, :]
                branch = dot(mixes[j][source, :], mixer_w[...]) + as_row(mixer_b)
                middle = xs[j][source, :].astype(F32) + mods[:, cut(2)] * branch
                normed_mid = layer_norm(middle)[0] * (1.0 + mods[:, cut(4)]) + mods[:, cut(3)]
                normed_mid = normed_mid.astype(BF16)
                output_grad = (mods[:, cut(5)] * cotangent(at)).astype(BF16)
                branch_scr[rows, :] = branch
                middle_scr[rows, :] = middle
                normed_scr[rows, :] = normed_mid
                grad_scr[rows, :] = output_grad
                normed_t[:, rows] = normed_mid.T
                grad_t[:, rows] = output_grad.T
                ob_acc[...] += column_sum(output_grad.astype(F32))

    units_of = pl.ds(pl.multiple_of(f * part, part), part)

    @pl.loop(0, total // STEP)
    def _(m):
        rows = pl.ds(pl.multiple_of(m * STEP * BLOCK, STEP * BLOCK), STEP * BLOCK)
        hidden = dot(normed_scr[rows, :], hidden_w[...]) + as_row(hidden_b)
        square = hidden * hidden
        bend = 0.7978845608028654 * 0.044715
        curve = jnp.tanh(hidden * (0.7978845608028654 + bend * square))
        half = 0.5 + 0.5 * curve
        active = (hidden * half).astype(BF16)
        slope = half + (0.5 * hidden) * (1.0 - curve * curve) * (
            0.7978845608028654 + 3.0 * bend * square
        )
        hidden_grad = (dot_nt(grad_scr[rows, :], output_w[...]) * slope).astype(BF16)
        out_acc[rows, :] += dot(active, output_w[...])
        mid_acc[rows, :] += dot_nt(hidden_grad, hidden_w[...])
        ow_acc[:, units_of] += dot(grad_t[:, rows], active)
        hw_acc[:, units_of] += dot(normed_t[:, rows], hidden_grad)
        hb_acc[:, units_of] += column_sum(hidden_grad.astype(F32))

    @pl.when(f == SPLIT - 1)
    def _():
        for j in range(u):

            for b in range(units[j][1]):
                source = pl.ds(b * BLOCK, BLOCK)
                at = b + lows[j]
                rows = pl.ds(at * BLOCK, BLOCK)
                mods = mods_ref[at : at + 1, :]
                gate_one, scale_two, gate_two = mods[:, cut(2)], mods[:, cut(4)], mods[:, cut(5)]
                middle, branch = middle_scr[rows, :], branch_scr[rows, :]
                cot = cotangent(at)
                output = out_acc[rows, :] + as_row(output_b)
                result = (middle + gate_two * output).astype(BF16)
                for s in range(n):
                    out_ref[s, at] = result[s * chunk : (s + 1) * chunk]
                normed, inverse = layer_norm(middle)
                mid_grad = mid_acc[rows, :]
                middle_grad = cot + norm_back(mid_grad * (1.0 + scale_two), normed, inverse)
                middle_out[rows, :] = middle_grad
                branch_grad = (gate_one * middle_grad).astype(BF16)
                mw_acc[...] += dot(mixes[j][source, :].T, branch_grad)
                mb_acc[...] += column_sum(branch_grad.astype(F32))
                mixed_grad_out[rows, :] = dot_nt(branch_grad, mixer_w[...]).astype(BF16)
                found = (
                    column_sum(middle_grad * branch),
                    column_sum(mid_grad),
                    column_sum(mid_grad * normed),
                    column_sum(cot * output),
                )
                for m, row in enumerate(found):
                    slots_acc[m, at : at + 1, :] = row

        ff = ow_acc.shape[1]
        rows_scr[:ff, :] = ow_acc[...].T.astype(BF16)
        for j in range(ff // width):
            lo = ff + j * width
            rows_scr[lo : lo + width, :] = hw_acc[:, j * width : (j + 1) * width].astype(BF16)
        if rows_scr.shape[0] > 2 * ff:
            rows_scr[2 * ff :, :] = jnp.zeros((rows_scr.shape[0] - 2 * ff, width), BF16)
        spread_out(me_ref, rows_scr.shape[0] // size, size, rows_scr, (first_out, second_out))
        mixer_out[...] = mw_acc[...]
        sums = [ob_acc[...]]
        sums += [hb_acc[:, j * width : (j + 1) * width] for j in range(ff // width)]
        sums += [mb_acc[...], jnp.zeros((8 - 2 - ff // width, width), F32)]
        small = [slots_acc[m] for m in range(4)] + [activity_ref[...]] + sums
        small_out[...] = jnp.concatenate(small, axis=0).astype(BF16)


def feed(units, n, chunk, size, me, valid, xs, mixes, cots, mods, activity, weights):
    width, ff = weights[2].shape
    total = sum(count for _, count in units)
    shape = jax.ShapeDtypeStruct
    tokens, part = total * BLOCK, ff // SPLIT
    arrays = [*xs, *mixes, cots, mods, activity, *weights]
    in_specs = [full(a.shape) for a in arrays]
    in_specs[-4] = pl.BlockSpec((width, part), lambda f: (0, f))
    in_specs[-3] = pl.BlockSpec((part,), lambda f: (f,))
    in_specs[-2] = pl.BlockSpec((part, width), lambda f: (f, 0))
    rows = padded(2 * ff, size)
    outs = [shape((n, total, chunk, width), BF16)]
    outs += [shape((tokens, width), F32), shape((tokens, width), BF16)]
    outs += [shape((rows // 2, width), BF16)] * 2
    outs += [shape((width, width), F32), shape((48, width), BF16)]
    in_specs, arrays = [SMEM] + in_specs, [me] + arrays
    if valid is not None:
        in_specs, arrays = [SMEM] + in_specs, [me, valid] + arrays[1:]
    found = pl.pallas_call(
        partial(feed_kernel, units, n, chunk, width, size, valid is not None),
        grid=(SPLIT,),
        in_specs=in_specs,
        out_specs=[full(o.shape) for o in outs],
        out_shape=outs,
        scratch_shapes=[
            pltpu.VMEM((tokens, width), F32),
            pltpu.VMEM((tokens, width), F32),
            pltpu.VMEM((tokens, width), F32),
            pltpu.VMEM((tokens, width), F32),
            pltpu.VMEM((tokens, width), BF16),
            pltpu.VMEM((tokens, width), BF16),
            pltpu.VMEM((width, tokens), BF16),
            pltpu.VMEM((width, tokens), BF16),
            pltpu.VMEM((width, ff), F32),
            pltpu.VMEM((width, ff), F32),
            pltpu.VMEM((width, width), F32),
            pltpu.VMEM((1, width), F32),
            pltpu.VMEM((1, ff), F32),
            pltpu.VMEM((1, width), F32),
            pltpu.VMEM((rows, width), BF16),
            pltpu.VMEM((4, 8, width), F32),
        ],
        compiler_params=params(),
        cost_estimate=cost(0.1),
        name="feed",
    )(*arrays)
    return found[0], found[1:]


def finish_kernel(units, n, chunk, width, count, *refs):
    u = len(units)
    total = sum(c for _, c in units)
    xs, refs = refs[:u], refs[u:]
    parts, weight_ref, refs = refs[: 3 * PAIRS], refs[3 * PAIRS], refs[3 * PAIRS + 1 :]
    if u > 1:
        own_ref, others, refs = refs[0], refs[1 : 1 + count], refs[1 + count :]
    sums, refs = refs[:PAIRS], refs[PAIRS:]
    middle_ref, mods_ref, out_ref, small_out, x_scr, g_scr, slots_acc = refs
    i = pl.program_id(0)

    @pl.when(i == 0)
    def _():
        slots_acc[...] = jnp.zeros_like(slots_acc)

    @pl.when(i < HALF)
    def _():
        x_scr[...] = xs[0][...]
        grads = jnp.concatenate([part[...] for part in parts], axis=1)
        g_scr[...] = dot_nt(grads, weight_ref[...])

    if u > 1:

        @pl.when(i >= HALF)
        def _():
            x_scr[...] = xs[1][...]
            grad = own_ref[...]
            for other in others:
                grad = grad + other[...].astype(F32)
            g_scr[...] = grad

    scale_one = mods_ref[pl.ds(i, 1), width : 2 * width]
    normed, inverse = layer_norm(x_scr[...].astype(F32))
    grad = g_scr[...]
    slots_acc[0, pl.ds(i, 1), :] = column_sum(grad)
    slots_acc[1, pl.ds(i, 1), :] = column_sum(grad * normed)
    result = middle_ref[...] + norm_back(grad * (1.0 + scale_one), normed, inverse)
    result = result.astype(BF16)
    for s in range(n):
        out_ref[s, 0] = result[s * chunk : (s + 1) * chunk]

    @pl.when(i == total - 1)
    def _():
        biases = [
            jnp.concatenate([ref[0:1, m * LANES : (m + 1) * LANES] for ref in sums], axis=1)
            for m in (0, 2)
        ]
        small = [slots_acc[0], slots_acc[1], *biases, jnp.zeros((14, width), F32)]
        small_out[...] = jnp.concatenate(small, axis=0).astype(BF16)


def finish(units, n, chunk, xs, parts, weight, own, others, sums, middle, mods):
    width = middle.shape[1]
    total = sum(count for _, count in units)
    shape = jax.ShapeDtypeStruct
    lows = [sum(count for _, count in units[:j]) for j in range(len(units))]

    def rows_of(j, columns):
        return pl.BlockSpec(
            (BLOCK, columns), lambda i: (jnp.clip(i - lows[j], 0, units[j][1] - 1), 0)
        )

    in_specs = [rows_of(j, width) for j in range(len(units))]
    in_specs += [rows_of(0, LANES)] * (3 * PAIRS) + [full(weight.shape)]
    arrays = [*xs, *parts, weight]
    if len(units) > 1:
        in_specs += [rows_of(1, width)] * (1 + len(others))
        arrays += [own, *others]
    in_specs += [full(s.shape) for s in sums]
    in_specs += [pl.BlockSpec((BLOCK, width), lambda i: (i, 0)), full(mods.shape)]
    arrays += [*sums, middle, mods]
    return pl.pallas_call(
        partial(finish_kernel, units, n, chunk, width, len(others)),
        grid=(total,),
        in_specs=in_specs,
        out_specs=[
            pl.BlockSpec((n, 1, chunk, width), lambda i: (0, i, 0, 0)),
            full((32, width)),
        ],
        out_shape=[shape((n, total, chunk, width), BF16), shape((32, width), BF16)],
        scratch_shapes=[
            pltpu.VMEM((BLOCK, width), BF16),
            pltpu.VMEM((BLOCK, width), F32),
            pltpu.VMEM((2, 8, width), F32),
        ],
        compiler_params=params(),
        cost_estimate=cost(0.1),
        name="finish",
    )(*arrays)


def settle_kernel(size, chunk, places, kept, me_ref, *refs):
    pieces, outs, small_out, rows_scr = refs[:kept], refs[kept:-2], refs[-2], refs[-1]
    held = pieces[0].shape[0] // (size // kept)
    for j, piece in enumerate(pieces):

        @pl.loop(0, size // kept)
        def _(p, j=j, piece=piece):
            at = pl.multiple_of(((p + j * (size // kept)) ^ me_ref[0]) * chunk, chunk)
            low = pl.multiple_of(p * held, 16)
            rows_scr[pl.ds(at, chunk), :] = piece[pl.ds(low, chunk), :].astype(F32)
            small_out[p + j * (size // kept)] = piece[pl.ds(low + chunk, held - chunk), :].astype(F32)

    width = rows_scr.shape[1]
    for out, low in zip(outs, places):
        rows = out.shape[0]
        for c in range(out.shape[1] // width):
            out[:, c * width : (c + 1) * width] = rows_scr[low + c * rows : low + (c + 1) * rows, :]


def settle(size, chunk, me, pieces, shapes):
    width = pieces[0].shape[1]
    held = pieces[0].shape[0] * len(pieces) // size
    places, low = [], 0
    for rows, columns in shapes:
        places.append(low)
        low += rows * (columns // width)
    shapes = [*shapes, (size, held - chunk, width)]
    return pl.pallas_call(
        partial(settle_kernel, size, chunk, places, len(pieces)),
        in_specs=[SMEM] + [full(h.shape) for h in pieces],
        out_specs=[full(s) for s in shapes],
        out_shape=[jax.ShapeDtypeStruct(s, F32) for s in shapes],
        grid=(1,),
        scratch_shapes=[pltpu.VMEM((size * chunk, width), F32)],
        compiler_params=params(40),
        cost_estimate=cost(0.1),
        name="settle",
    )(me, *pieces)


def modulate_kernel(early_ref, late_ref, *refs):
    size, _, width = early_ref.shape
    weight_out, bias_out, early_out, late_out = refs
    flat = lambda ref, m: ref[:, 8 * m : 8 * (m + 1), :].reshape(size * 8, width)
    activity = flat(early_ref, 4).astype(BF16).T
    for m in range(6):
        slots = flat(late_ref, m) if m < 2 else flat(early_ref, m - 2)
        lanes = slice(m * width, (m + 1) * width)
        weight_out[:, lanes] = dot(activity, slots.astype(BF16))
        bias_out[:, lanes] = column_sum(slots)
    early_out[...] = jnp.sum(early_ref[:, 40:48, :], axis=0)
    late_out[...] = jnp.sum(late_ref[:, 16:24, :], axis=0)


def modulate(early, late):
    width = early.shape[2]
    shapes = [(width, 6 * width), (1, 6 * width), (8, width), (8, width)]
    return pl.pallas_call(
        modulate_kernel,
        out_shape=[jax.ShapeDtypeStruct(s, F32) for s in shapes],
        compiler_params=params(40),
        cost_estimate=cost(0.1),
        name="modulate",
    )(early, late)


def xor_permute(value, mask, size):
    return lax.ppermute(value, ("rows", "band"), [(i, i ^ mask) for i in range(size)])


def stages_of(rows, bands):
    band_bits, bits = bands.bit_length() - 1, (rows * bands).bit_length() - 1
    stages = [[band_bits]]
    for low, high in ((band_bits + 1, bits), (0, band_bits)):
        if (high - low) % 2:
            stages.append([low])
            low += 1
        stages += [[b, b + 1] for b in range(low, high, 2)]
    return stages


def digit_of(me, stage):
    return sum(((me >> b) & 1) << i for i, b in enumerate(stage))


def mask_of(t, stage):
    return sum(((t >> i) & 1) << b for i, b in enumerate(stage))


def fold_kernel(count, *refs):
    total = refs[0][...].astype(F32)
    for ref in refs[1:count]:
        total = total + ref[...].astype(F32)
    outs = refs[count:]
    rows = total.shape[0] // len(outs)
    for j, out in enumerate(outs):
        out[...] = total[j * rows : (j + 1) * rows].astype(BF16)


def fold(arrays, parts):
    rows, width = arrays[0].shape
    shape = jax.ShapeDtypeStruct((rows // parts, width), BF16)
    found = pl.pallas_call(
        partial(fold_kernel, len(arrays)),
        out_shape=[shape] * parts,
        compiler_params=params(32),
        cost_estimate=cost(0.1),
        name="fold",
    )(*arrays)
    return list(found)


def after(value, *others):
    return lax.optimization_barrier((value, others))[0]


def join_kernel(count, *refs):
    rows = refs[0].shape[0]
    for j in range(count):
        refs[count][j * rows : (j + 1) * rows, :] = refs[j][...]


def join(arrays):
    rows, width = arrays[0].shape
    return pl.pallas_call(
        partial(join_kernel, len(arrays)),
        out_shape=jax.ShapeDtypeStruct((rows * len(arrays), width), BF16),
        compiler_params=params(32),
        cost_estimate=cost(0.1),
        name="join",
    )(*arrays)


class Sum:
    def __init__(self, stages, size, parts):
        self.stages, self.size, self.at = stages, size, 0
        self.scattered = False
        self.steps = self.left = 2 * len(stages) - 1
        self.send(parts)

    def send(self, parts):
        stage = self.stages[self.at]
        self.held = [parts[0]] + [
            xor_permute(part, mask_of(t, stage), self.size) for t, part in enumerate(parts) if t
        ]

    def step(self, extra=None, done=()):
        held = list(after(self.held, *done)) if done else self.held
        self.left -= 1
        self.at += -1 if self.scattered else 1
        if not self.scattered and self.at < len(self.stages):
            parts = fold(held, 1 << len(self.stages[self.at]))
            self.send(parts)
            return parts
        if not self.scattered:
            self.scattered = True
            self.at -= 1
            value = fold(held, 1)[0]
            if extra is not None:
                value = jnp.concatenate([value, extra], axis=0)
        else:
            value = join(held)
        self.send([value] * (1 << len(self.stages[self.at])))
        return [value]


def body(
    patches,
    condition_table,
    condition_index,
    image_lengths,
    modulate_weight,
    modulate_bias,
    triple_weight,
    query_bias,
    value_bias,
    mixer_weight,
    mixer_bias,
    hidden_weight,
    hidden_bias,
    output_weight,
    output_bias,
    cotangent,
):
    band = lax.axis_index("band")
    n = lax.axis_size("band")
    size = n * lax.axis_size("rows")
    everyone = lax.axis_index(("rows", "band"))
    rows, band_length, width = patches.shape
    ff = hidden_weight.shape[1]
    length = band_length * n
    big = length // 2
    chunk = band_length // (2 * HALF)
    assert length == 2 * HALF * BLOCK
    plan = Plan(rows, n)
    units, total = plan.units(), plan.total
    assert units[0][1] == HALF
    stages = stages_of(size // n, n)
    relative = jnp.int32(0)
    for stage in stages:
        relative = (relative << len(stage)) | digit_of(everyone, stage)
    relative = relative.astype(jnp.int32).reshape(1)

    def deal(pieces):
        return lax.all_to_all(pieces, "band", 0, 0, tiled=True)

    me = band.astype(jnp.int32).reshape(1)
    packed = pack(plan, chunk, big, me, image_lengths, patches, True)
    x_pieces = [p if s == 0 else xor_permute(p, s, size) for s, p in enumerate(packed)]

    mods, activity, flags = prepare(
        plan,
        big,
        me,
        image_lengths,
        condition_index,
        condition_table,
        modulate_weight,
        modulate_bias,
    )
    c_pieces = deal(pack(plan, chunk, big, me, image_lengths, after(cotangent, mods, x_pieces[1:TIE]), False))

    attended, xs, mixes = [], [], []
    others = [[] for _ in units]
    if plan.group > 1:
        own = collect(n, plan.whole * HALF, plan.own, chunk, me, x_pieces)
        others[-1] = [xor_permute(own, t, size) for t in range(1, plan.group)]
    for j, (name, count) in enumerate(units):
        lo = j * HALF
        found = attend(
            n,
            j,
            lo,
            count,
            HALF,
            chunk,
            me,
            flags,
            x_pieces,
            others[j],
            mods,
            triple_weight,
            query_bias,
            value_bias,
        )
        xs.append(found[0])
        attended.append(found[1:8])
        mixes.append(found[8])

    valid = None
    if plan.idle:
        valid = (plan.half_row("shared", band) < plan.halves).astype(F32).reshape(1)

    weights = [
        mixer_weight,
        mixer_bias,
        hidden_weight,
        hidden_bias,
        output_weight,
        output_bias,
    ]
    out_pieces, fed = feed(
        units,
        n,
        chunk,
        size,
        relative,
        valid,
        xs,
        mixes,
        c_pieces,
        mods,
        activity,
        weights,
    )
    middle_grad, mixed_grad, first, second, mixer_grad, feed_small = fed
    out_back = deal(out_pieces)
    feed_sum = Sum(stages, size, [first, second])

    own, others, begun = None, [], []
    token = feed_sum.step()
    mixed_grad = after(mixed_grad, *token)
    if len(units) > 1:
        kept, low = attended[1], HALF
        found = shared_back(units[1][1], HALF, flags, kept, mixed_grad, low, triple_weight)
        own, others = found[0], [xor_permute(o, t + 1, size) for t, o in enumerate(found[1:-2])]
        begun = found[-2:]
        token = feed_sum.step(feed_small, done=(own,))
    grouped, sums, earlier = [], [], []
    for p in range(PAIRS):
        grad = after(mixed_grad, *token, *(others if p == 1 else []))
        found = whole_back(
            size, relative, p, flags, attended[0], grad, begun, mixer_grad, earlier
        )
        grouped.append(found[:3])
        sums.append(found[3])
        if p < PAIRS - 1:
            earlier.append(found[4])
            token = feed_sum.step(feed_small, done=(found[0],))
    last_sum = Sum(stages, size, found[4:6])
    token = feed_sum.step(feed_small, done=(found[3],))
    parts = [grouped[p][m] for m in range(3) for p in range(PAIRS)]
    grad_pieces, last_small = finish(
        units,
        n,
        chunk,
        xs,
        parts,
        triple_weight,
        own,
        others,
        sums,
        after(middle_grad, out_back, *token),
        mods,
    )
    grad_back = deal(grad_pieces)
    feed_chunk, last_chunk = (padded(r, size) // size for r in (2 * ff, 4 * width))
    last_sum.step(last_small, done=(last_small,))
    while feed_sum.left:
        token = feed_sum.step(feed_small, done=token)
    block_out = unpack(plan, chunk, big, image_lengths, out_back, BF16)
    output_w_grad, hidden_w_grad, early = settle(
        size, feed_chunk, relative, feed_sum.held, [(ff, width), (width, ff)]
    )
    patch_grad = unpack(plan, chunk, big, image_lengths, grad_back, F32)
    while last_sum.left:
        token = ()
        if last_sum.left == 2:
            token = (grad_back, block_out, output_w_grad)
        if last_sum.left == 1:
            token = (patch_grad,)
        last_sum.step(last_small, done=token)
    triple_w_grad, mixer_w_grad, late = settle(
        size, last_chunk, relative, last_sum.held, [(width, 3 * width), (width, width)]
    )
    modulate_w_grad, modulate_b_grad, feed_sums, last_sums = modulate(early, late)
    return (
        block_out,
        patch_grad,
        modulate_w_grad,
        modulate_b_grad.reshape(-1),
        triple_w_grad,
        last_sums[0],
        last_sums[1],
        mixer_w_grad,
        feed_sums[1 + ff // width],
        hidden_w_grad,
        feed_sums[1 : 1 + ff // width].reshape(-1),
        output_w_grad,
        feed_sums[0],
    )


def solution(mesh):
    return jax.shard_map(
        body,
        mesh=mesh,
        in_specs=(
            P("rows", None, "band"),
            P(),
            P("rows", None),
            P("rows", None),
            P(),
            P(),
            P(),
            P(),
            P(),
            P(),
            P(),
            P(),
            P(),
            P(),
            P(),
            P("rows", None, "band"),
        ),
        out_specs=(
            P("rows", None, "band"),
            P("rows", None, "band"),
            P(),
            P(),
            P(),
            P(),
            P(),
            P(),
            P(),
            P(),
            P(),
            P(),
            P(),
        ),
        check_vma=False,
    )
```

```python
from functools import partial

import jax
import jax.numpy as jnp
from jax import lax
from jax.experimental import pallas as pl
from jax.experimental.pallas import tpu as pltpu
from jax.sharding import PartitionSpec as P

HEADS = 6
HEAD_DIM = 64
PAIRS = HEADS // 2
LANES = 128
BLOCK = 256
HALF = 4
EPSILON = 1e-06
ONES = 16
TIE = 8
F32 = jnp.float32
BF16 = jnp.bfloat16
MIB = 1 << 20


def dot(left, right):
    return jnp.dot(left, right, preferred_element_type=F32)


def dot_nt(left, right):
    return lax.dot_general(left, right, (((1,), (1,)), ((), ())), preferred_element_type=F32)


def params(limit=56, **more):
    return pltpu.CompilerParams(vmem_limit_bytes=limit * MIB, **more)


def cost(micros):
    return pl.CostEstimate(flops=0, bytes_accessed=int(micros * 3e6), transcendentals=0)


def full(shape):
    return pl.BlockSpec(shape, lambda *_: (0,) * len(shape))


SMEM = pl.BlockSpec(memory_space=pltpu.SMEM)


def row_layout(lens_ref, row, slots, big):
    count = jnp.int32(0)
    before = jnp.int32(0)
    for j in range(slots):
        is_big = (lens_ref[row, j] == big).astype(jnp.int32)
        before = before + jnp.where(count + is_big == 0, 1, 0)
        count = count + is_big
    return count, jnp.where(count == 1, before, 0)


def chunk_of(start, half, k):
    return jnp.where(half == 0, start + k, jnp.where(k < start, k, k + HALF))


class Plan:
    def __init__(self, rows, bands):
        self.rows, self.bands = rows, bands
        self.halves = 2 * rows
        self.whole = self.halves // bands
        assert self.whole <= 1
        self.rest = self.halves - self.whole * bands
        self.group = 1
        while self.rest and self.rest * self.group * 2 <= bands and self.group < HALF:
            self.group *= 2
        self.idle = self.rest * self.group != bands
        self.own = HALF // self.group

    @property
    def total(self):
        return sum(count for _, count in self.units())

    def units(self):
        found = []
        if self.whole:
            found.append(("whole", HALF))
        if self.rest:
            found.append(("shared", self.own))
        return found

    def half_row(self, name, device):
        if name == "whole":
            return device
        return self.whole * self.bands + device // self.group

    def first(self, name, device):
        return 0 if name == "whole" else (device % self.group) * self.own


def pack_kernel(plan, chunk, slots, big, apart, me_ref, lens_ref, x_ref, *outs):
    for s in range(plan.bands):
        dest = me_ref[0] ^ s if apart else s
        at = 0
        for name, count in plan.units():
            half_row = jnp.minimum(plan.half_row(name, dest), plan.halves - 1)
            row, half = half_row // 2, half_row % 2
            start = row_layout(lens_ref, row, slots, big)[1]
            for k in range(count):
                source = chunk_of(start, half, plan.first(name, dest) + k)
                rows = pl.ds(pl.multiple_of(source * chunk, chunk), chunk)
                if apart:
                    outs[s][at] = x_ref[row, rows, :]
                else:
                    outs[0][dest, at] = x_ref[row, rows, :]
                at += 1


def pack(plan, chunk, big, me, lens, x, apart):
    shape = (plan.total, chunk, x.shape[2])
    shapes = [shape] * plan.bands if apart else [(plan.bands,) + shape]
    found = pl.pallas_call(
        partial(pack_kernel, plan, chunk, lens.shape[1], big, apart),
        in_specs=[SMEM, SMEM, full(x.shape)],
        out_specs=[full(s) for s in shapes],
        out_shape=[jax.ShapeDtypeStruct(s, x.dtype) for s in shapes],
        grid=(1,),
        compiler_params=params(32),
        cost_estimate=cost(0.1),
        name="pack",
    )(me, lens, x)
    return found if apart else found[0]


def unpack_kernel(plan, chunk, slots, big, lens_ref, piece_ref, out_ref):
    for owner in range(plan.bands):
        at = 0
        for name, count in plan.units():
            half_row = plan.half_row(name, owner)
            if half_row < plan.halves:
                row, half = half_row // 2, half_row % 2
                start = row_layout(lens_ref, row, slots, big)[1]
                for k in range(count):
                    source = chunk_of(start, half, plan.first(name, owner) + k)
                    rows = pl.ds(pl.multiple_of(source * chunk, chunk), chunk)
                    out_ref[row, rows, :] = piece_ref[owner, at + k].astype(out_ref.dtype)
            at += count


def unpack(plan, chunk, big, lens, pieces, dtype):
    shape = (plan.rows, chunk * 2 * HALF, pieces.shape[3])
    return pl.pallas_call(
        partial(unpack_kernel, plan, chunk, lens.shape[1], big),
        in_specs=[SMEM, full(pieces.shape)],
        out_specs=full(shape),
        out_shape=jax.ShapeDtypeStruct(shape, dtype),
        grid=(1,),
        compiler_params=params(32),
        cost_estimate=cost(0.1),
        name="unpack",
    )(lens, pieces)


def collect_kernel(n, low, count, chunk, me_ref, *refs):
    for b in range(count):
        for s in range(n):
            at = pl.multiple_of(b * BLOCK + (me_ref[0] ^ s) * chunk, chunk)
            refs[n][pl.ds(at, chunk), :] = refs[s][low + b]


def collect(n, low, count, chunk, me, pieces):
    width = pieces[0].shape[2]
    return pl.pallas_call(
        partial(collect_kernel, n, low, count, chunk),
        in_specs=[SMEM] + [full(p.shape) for p in pieces],
        out_specs=full((count * BLOCK, width)),
        out_shape=jax.ShapeDtypeStruct((count * BLOCK, width), BF16),
        grid=(1,),
        compiler_params=params(16),
        cost_estimate=cost(0.1),
        name="collect",
    )(me, *pieces)


def prepare_kernel(plan, slots, big, me_ref, lens_ref, index_ref, table_ref, weight_ref, bias_ref, *refs):
    mods_out, activity_out, flags_out, table_scr, activity_scr = refs
    table_scr[...] = table_ref[...].astype(F32)
    activity_scr[...] = jnp.zeros_like(activity_scr)
    at = 0
    for j, (name, count) in enumerate(plan.units()):
        half_row = jnp.minimum(plan.half_row(name, me_ref[0]), plan.halves - 1)
        row, half = half_row // 2, half_row % 2
        bigs, start = row_layout(lens_ref, row, slots, big)
        is_big = jnp.logical_or(bigs == 2, jnp.logical_and(bigs == 1, half == 0))
        flags_out[j] = is_big.astype(jnp.int32)
        for t in range(HALF // count):
            first = 0 if count == HALF else ((me_ref[0] % plan.group) ^ t) * count
            for k in range(count):
                place = first + k
                single = jnp.where(half == 0, start, jnp.where(place < start, place, place + 1))
                slot = jnp.where(bigs == 2, half, jnp.where(bigs == 0, HALF * half + place, single))
                chosen = table_scr[pl.ds(index_ref[row, slot], 1), :]
                activity_scr[at : at + 1, :] = chosen * (1.0 / (1.0 + jnp.exp(-chosen)))
                at += 1
    activity = activity_scr[...].astype(BF16)
    activity_out[...] = activity.astype(F32)
    mods_out[...] = dot(activity, weight_ref[...]) + as_row(bias_ref)


def prepare(plan, big, me, lens, index, table, weight, bias):
    width = table.shape[1]
    shape = jax.ShapeDtypeStruct
    arrays = [table, weight, bias]
    return pl.pallas_call(
        partial(prepare_kernel, plan, lens.shape[1], big),
        in_specs=[SMEM] * 3 + [full(a.shape) for a in arrays],
        out_specs=[full((8, weight.shape[1])), full((8, width)), SMEM],
        out_shape=[
            shape((8, weight.shape[1]), F32),
            shape((8, width), F32),
            shape((2,), jnp.int32),
        ],
        grid=(1,),
        scratch_shapes=[pltpu.VMEM(table.shape, F32), pltpu.VMEM((8, width), F32)],
        compiler_params=params(32),
        cost_estimate=cost(0.1),
        name="prepare",
    )(me, lens, index, *arrays)


def layer_norm(values):
    centre = values - jnp.mean(values, axis=-1, keepdims=True)
    inverse = lax.rsqrt(jnp.mean(centre * centre, axis=-1, keepdims=True) + EPSILON)
    return centre * inverse, inverse


def norm_back(grad, normed, inverse):
    return inverse * (
        grad
        - jnp.mean(grad, axis=-1, keepdims=True)
        - normed * jnp.mean(grad * normed, axis=-1, keepdims=True)
    )


def as_row(ref):
    return ref[...].astype(F32).reshape(1, -1)


def column_sum(values):
    return jnp.sum(values, axis=0, keepdims=True)


def attend_kernel(n, unit, low, nq, nk, chunk, width, me_ref, flag_ref, *refs):
    pieces, refs = refs[:n], refs[n:]
    count = nk // nq - 1
    others, refs = refs[:count], refs[count:]
    mods_ref, weight_ref, query_bias_ref, value_bias_ref = refs[:4]
    x_out, hint_out, q_out, k_out, v_out, e_out, ot_out, inv_out, mixed_out = refs[4:13]
    k_scr, qt_scr, vt_scr = refs[13:]
    p = pl.program_id(0)

    @pl.when(p == 0)
    def _():
        qt_scr[...] = jnp.zeros_like(qt_scr)
        for h in range(HEADS):
            vt_scr[h, HEAD_DIM:, :] = jnp.ones((ONES, nk * BLOCK), BF16)
        for b in range(nk):
            rows = pl.ds(b * BLOCK, BLOCK)
            if b < nq:
                for s in range(n):
                    at = pl.multiple_of(b * BLOCK + (me_ref[0] ^ s) * chunk, chunk)
                    x_out[pl.ds(at, chunk), :] = pieces[s][low + b]
            else:
                t, inner = b // nq - 1, b % nq
                x_out[rows, :] = others[t][pl.ds(inner * BLOCK, BLOCK), :]
            source = x_out[rows, :].astype(F32)
            normed = layer_norm(source)[0]
            shift = mods_ref[low + b : low + b + 1, 0:width]
            scale = mods_ref[low + b : low + b + 1, width : 2 * width]
            hin = (normed * (1.0 + scale) + shift).astype(BF16)
            hint_out[:, rows] = hin.T
            triple = dot(hin, weight_ref[...])
            keys = triple[:, width : 2 * width].astype(BF16)
            values = (triple[:, 2 * width :] + as_row(value_bias_ref)).astype(BF16)
            values_t = values.T
            for j in range(PAIRS):
                lanes = slice(j * LANES, (j + 1) * LANES)
                k_scr[j, rows, :] = keys[:, lanes]
                k_out[j, rows, :] = keys[:, lanes]
                v_out[j, rows, :] = values[:, lanes]
            for h in range(HEADS):
                vt_scr[h, :HEAD_DIM, rows] = values_t[h * HEAD_DIM : (h + 1) * HEAD_DIM]
            if b < nq:
                query = (triple[:, :width] + as_row(query_bias_ref)) * (HEAD_DIM**-0.5)
                query = query.astype(BF16)
                for j in range(PAIRS):
                    q_out[j, rows, :] = query[:, j * LANES : (j + 1) * LANES]
                query_t = query.T
                for h in range(HEADS):
                    to = (h % 2) * HEAD_DIM
                    qt_scr[h, to : to + HEAD_DIM, rows] = query_t[
                        h * HEAD_DIM : (h + 1) * HEAD_DIM
                    ]

    def tile(columns, krows):
        found = []
        for hh in range(2):
            h = 2 * p + hh
            scores = dot(k_scr[p, krows, :], qt_scr[h, :, columns])
            exps = jnp.exp(scores - jnp.max(scores, axis=0, keepdims=True)).astype(BF16)
            e_out[hh, krows, columns] = exps
            summed = dot(vt_scr[h, :, krows], exps)
            inverse = 1.0 / summed[HEAD_DIM : HEAD_DIM + 1]
            found.append(summed[:HEAD_DIM] * inverse)
            inv_out[0, hh : hh + 1, columns] = inverse
        both = jnp.concatenate(found, axis=0)
        ot_out[0, :, columns] = both
        mixed_out[columns, :] = both.T.astype(BF16)

    @pl.when(flag_ref[unit] == 1)
    def _():
        tile(pl.ds(0, nq * BLOCK), pl.ds(0, nk * BLOCK))

    @pl.when(flag_ref[unit] == 0)
    def _():
        for b in range(nq):
            tile(pl.ds(b * BLOCK, BLOCK), pl.ds(b * BLOCK, BLOCK))


def attend(n, unit, low, nq, nk, chunk, me, flag, pieces, others, mods, weight, query_bias, value_bias):
    width = weight.shape[0]
    qs, ks = nq * BLOCK, nk * BLOCK
    shape = jax.ShapeDtypeStruct
    outs = [
        (shape((ks, width), BF16), None),
        (shape((width, ks), BF16), None),
        (shape((PAIRS, qs, LANES), BF16), None),
        (shape((PAIRS, ks, LANES), BF16), None),
        (shape((PAIRS, ks, LANES), BF16), None),
        (shape((HEADS, ks, qs), BF16), pl.BlockSpec((2, ks, qs), lambda p: (p, 0, 0))),
        (shape((PAIRS, LANES, qs), F32), pl.BlockSpec((1, LANES, qs), lambda p: (p, 0, 0))),
        (shape((PAIRS, 8, qs), F32), pl.BlockSpec((1, 8, qs), lambda p: (p, 0, 0))),
        (shape((qs, width), BF16), pl.BlockSpec((qs, LANES), lambda p: (0, p))),
    ]
    arrays = [*pieces, *others, mods, weight, query_bias, value_bias]
    flops = 2 * ks * width * 3 * width + 4 * HEADS * qs * ks * HEAD_DIM * 4
    return pl.pallas_call(
        partial(attend_kernel, n, unit, low, nq, nk, chunk, width),
        grid=(PAIRS,),
        in_specs=[SMEM, SMEM] + [full(a.shape) for a in arrays],
        out_specs=[spec or full(s.shape) for s, spec in outs],
        out_shape=[s for s, _ in outs],
        scratch_shapes=[
            pltpu.VMEM((PAIRS, ks, LANES), BF16),
            pltpu.VMEM((HEADS, LANES, qs), BF16),
            pltpu.VMEM((HEADS, HEAD_DIM + ONES, ks), BF16),
        ],
        compiler_params=params(),
        cost_estimate=cost(0.1),
        name="attend",
    )(me, flag, *arrays)


def back_tile(qlow, qsize, klow, ksize, e_ref, q_ref, k_ref, v_ref, ot_ref, inv_ref, grad_ref):
    columns, krows = pl.ds(qlow, qsize), pl.ds(klow, ksize)
    lane = lax.broadcasted_iota(jnp.int32, (qsize, LANES), 1)
    grad_t = grad_ref[columns, :].astype(F32).T
    keys_t = k_ref[0, krows, :].T
    query = q_ref[0, columns, :]
    zeros = jnp.zeros((HEAD_DIM, qsize), BF16)
    found, keys_grad, values_grad = [], None, None
    for hh in range(2):
        part = slice(hh * HEAD_DIM, (hh + 1) * HEAD_DIM)
        scaled = (grad_t[part] * inv_ref[0, hh : hh + 1, columns]).astype(BF16)
        delta = column_sum(scaled.astype(F32) * ot_ref[0, part, columns])
        masked = jnp.concatenate([scaled, zeros] if hh == 0 else [zeros, scaled], axis=0)
        exps = e_ref[hh, krows, columns]
        prob_grad = dot(v_ref[0, krows, :], masked)
        score_grad = (exps.astype(F32) * (prob_grad - delta)).astype(BF16)
        own = (lane < HEAD_DIM) if hh == 0 else (lane >= HEAD_DIM)
        values_part = dot_nt(exps, masked)
        keys_part = dot(score_grad, jnp.where(own, query, jnp.zeros_like(query)))
        values_grad = values_part if hh == 0 else values_grad + values_part
        keys_grad = keys_part if hh == 0 else keys_grad + keys_part
        found.append(dot(keys_t[part], score_grad))
    both = jnp.concatenate(found, axis=0) * (HEAD_DIM**-0.5)
    return both.T.astype(BF16), keys_grad.astype(BF16), values_grad.astype(BF16)


def shared_back_kernel(nq, nk, flag_ref, *refs):
    tile_refs, (hint_ref, weight_ref, own_out), refs = refs[:7], refs[7:10], refs[10:]
    others_out, (tw_out, tb_out, tg_scr) = refs[:-3], refs[-3:]
    p = pl.program_id(0)
    qs, rest = nq * BLOCK, (nk - nq) * BLOCK

    def tile(qlow, qsize, klow, ksize):
        query_grad, keys_grad, values_grad = back_tile(qlow, qsize, klow, ksize, *tile_refs)
        tg_scr[p, pl.ds(qlow, qsize), :] = query_grad
        tg_scr[PAIRS + p, pl.ds(klow, ksize), :] = keys_grad
        tg_scr[2 * PAIRS + p, pl.ds(klow, ksize), :] = values_grad

    tg_scr[p, qs:, :] = jnp.zeros((rest, LANES), BF16)

    @pl.when(flag_ref[1] == 1)
    def _():
        tile(0, qs, 0, nk * BLOCK)

    @pl.when(flag_ref[1] == 0)
    def _():
        for j in (1, 2):
            tg_scr[j * PAIRS + p, qs:, :] = jnp.zeros((rest, LANES), BF16)
        for b in range(nq):
            tile(b * BLOCK, BLOCK, b * BLOCK, BLOCK)

    @pl.when(p == PAIRS - 1)
    def _():
        grads = jnp.concatenate([tg_scr[j] for j in range(3 * PAIRS)], axis=1)
        back = dot_nt(grads, weight_ref[...])
        own_out[...] = back[:qs]
        for t, out in enumerate(others_out):
            out[...] = back[(t + 1) * qs : (t + 2) * qs].astype(BF16)
        weight_grad = dot(hint_ref[...], grads)
        sums = column_sum(grads.astype(F32))
        for j in range(PAIRS):
            for m in range(3):
                low = (m * PAIRS + j) * LANES
                tw_out[j, :, m * LANES : (m + 1) * LANES] = weight_grad[:, low : low + LANES]
                tb_out[j, :, m * LANES : (m + 1) * LANES] = jnp.broadcast_to(
                    sums[:, low : low + LANES], (8, LANES)
                )


def whole_back_kernel(size, begun, flag_ref, *refs):
    tile_refs, hint_ref, refs = refs[:7], refs[7], refs[8:]
    if begun:
        tw_ref, tb_ref, refs = refs[0], refs[1], refs[2:]
    me_ref, mixer_ref, tq_out, tk_out, tv_out, tb_out, first_out, second_out, rows_scr = refs
    p = pl.program_id(0)

    def tile(qlow, qsize, klow, ksize):
        query_grad, keys_grad, values_grad = back_tile(qlow, qsize, klow, ksize, *tile_refs)
        tq_out[0, pl.ds(qlow, qsize), :] = query_grad
        tk_out[0, pl.ds(klow, ksize), :] = keys_grad
        tv_out[0, pl.ds(klow, ksize), :] = values_grad

    @pl.when(flag_ref[0] == 1)
    def _():
        tile(0, HALF * BLOCK, 0, HALF * BLOCK)

    @pl.when(flag_ref[0] == 0)
    def _():
        for b in range(HALF):
            tile(b * BLOCK, BLOCK, b * BLOCK, BLOCK)

    grads = jnp.concatenate([tq_out[0], tk_out[0], tv_out[0]], axis=1)
    weight_grad = dot(hint_ref[...], grads)
    sums = column_sum(grads.astype(F32))
    if begun:
        weight_grad, sums = weight_grad + tw_ref[0], sums + tb_ref[0, 0:1]
    tb_out[0] = jnp.broadcast_to(sums, tb_out.shape[1:])
    width = weight_grad.shape[0]
    lanes = pl.ds(pl.multiple_of(p * LANES, LANES), LANES)
    for m in range(3):
        rows_scr[m * width : (m + 1) * width, lanes] = weight_grad[
            :, m * LANES : (m + 1) * LANES
        ].astype(BF16)

    @pl.when(p == PAIRS - 1)
    def _():
        rows_scr[3 * width : 4 * width, :] = mixer_ref[...].astype(BF16)
        if rows_scr.shape[0] > 4 * width:
            rows_scr[4 * width :, :] = jnp.zeros((rows_scr.shape[0] - 4 * width, width), BF16)
        spread_out(me_ref, rows_scr.shape[0] // size, size, rows_scr, (first_out, second_out))


def back_inputs(nq, nk, first, flag, kept, grad, low):
    hint, q, k, v, e, ot, inv = kept
    qs, ks = nq * BLOCK, nk * BLOCK
    by_pair = lambda *tail: pl.BlockSpec((1,) + tail, lambda p: (first + p, 0, 0))
    in_specs = [
        SMEM,
        pl.BlockSpec((2, ks, qs), lambda p: (first + p, 0, 0)),
        by_pair(qs, LANES),
        by_pair(ks, LANES),
        by_pair(ks, LANES),
        by_pair(LANES, qs),
        by_pair(8, qs),
        pl.BlockSpec((qs, LANES), lambda p: (low * BLOCK // qs, first + p)),
        full(hint.shape),
    ]
    return in_specs, [flag, e, q, k, v, ot, inv, grad, hint]


def back_cost(qs, ks, steps):
    flops = 8 * 2 * steps * qs * ks * HEAD_DIM * 4
    return pl.CostEstimate(flops=flops, bytes_accessed=4 * steps * qs * ks, transcendentals=0)


def shared_back(nq, nk, flag, kept, grad, low, weight):
    width = weight.shape[0]
    qs, ks = nq * BLOCK, nk * BLOCK
    in_specs, arrays = back_inputs(nq, nk, 0, flag, kept, grad, low)
    shape = jax.ShapeDtypeStruct
    outs = [shape((qs, width), F32)] + [shape((qs, width), BF16)] * (nk // nq - 1)
    outs += [shape((PAIRS, width, 3 * LANES), F32), shape((PAIRS, 8, 3 * LANES), F32)]
    return pl.pallas_call(
        partial(shared_back_kernel, nq, nk),
        grid=(PAIRS,),
        in_specs=in_specs + [full(weight.shape)],
        out_specs=[full(o.shape) for o in outs],
        out_shape=outs,
        scratch_shapes=[pltpu.VMEM((3 * PAIRS, ks, LANES), BF16)],
        compiler_params=params(),
        cost_estimate=cost(0.1),
        name="shared_back",
    )(*arrays, weight)


def whole_back(size, me, flag, kept, grad, begun, mixer):
    width = mixer.shape[0]
    rows = HALF * BLOCK
    in_specs, arrays = back_inputs(HALF, HALF, 0, flag, kept, grad, 0)
    shape = jax.ShapeDtypeStruct
    if begun:
        in_specs += [pl.BlockSpec((1,) + b.shape[1:], lambda p: (p, 0, 0)) for b in begun]
        arrays += begun
    in_specs += [SMEM, full(mixer.shape)]
    arrays += [me, mixer]
    total = padded(4 * width, size)
    pairs = [shape((PAIRS, rows, LANES), BF16)] * 3 + [shape((PAIRS, 8, 3 * LANES), F32)]
    outs = pairs + [shape((total // 2, width), BF16)] * 2
    out_specs = [pl.BlockSpec((1,) + o.shape[1:], lambda p: (p, 0, 0)) for o in pairs]
    return pl.pallas_call(
        partial(whole_back_kernel, size, bool(begun)),
        grid=(PAIRS,),
        in_specs=in_specs,
        out_specs=out_specs + [full(o.shape) for o in outs[4:]],
        out_shape=outs,
        scratch_shapes=[pltpu.VMEM((total, width), BF16)],
        compiler_params=params(),
        cost_estimate=cost(0.1),
        name="whole_back",
    )(*arrays)


def spread_out(me_ref, chunk, size, source, outs):
    half = size // 2
    for j, out in enumerate(outs):

        @pl.loop(0, half)
        def _(p, j=j, out=out):
            at = pl.multiple_of(((p + j * half) ^ me_ref[0]) * chunk, chunk)
            out[pl.ds(pl.multiple_of(p * chunk, chunk), chunk), :] = source[pl.ds(at, chunk), :]


def padded(rows, size):
    return rows + -rows % (16 * size)


STEP = 6
SPLIT = 1


def feed_kernel(units, n, chunk, width, size, masked, me_ref, *refs):
    total = sum(count for _, count in units)
    u = len(units)
    if masked:
        valid_ref, refs = refs[0], refs[1:]
    xs, mixes, cot_ref, refs = refs[:u], refs[u : 2 * u], refs[2 * u], refs[2 * u + 1 :]
    mods_ref, activity_ref, mixer_w, mixer_b, hidden_w, hidden_b, output_w, output_b = refs[:8]
    out_ref, refs = refs[8], refs[9:]
    middle_out, mixed_grad_out, first_out, second_out, mixer_out, small_out, refs = *refs[:6], refs[6:]
    middle_scr, branch_scr, out_acc, mid_acc, normed_scr, grad_scr, normed_t, grad_t = refs[:8]
    ow_acc, hw_acc, mw_acc, ob_acc, hb_acc, mb_acc, rows_scr, slots_acc = refs[8:]
    f = pl.program_id(0)
    part = ow_acc.shape[1] // SPLIT
    cut = lambda at: slice(at * width, (at + 1) * width)
    lows = [sum(count for _, count in units[:j]) for j in range(u)]

    def cotangent(b):
        cot = jnp.concatenate([cot_ref[s, b] for s in range(n)], axis=0).astype(F32)
        return cot * valid_ref[0] if masked else cot

    @pl.when(f == 0)
    def _():
        for acc in (out_acc, mid_acc, ow_acc, hw_acc, mw_acc, ob_acc, hb_acc, mb_acc, slots_acc):
            acc[...] = jnp.zeros_like(acc)
        for j in range(u):

            for b in range(units[j][1]):
                source = pl.ds(b * BLOCK, BLOCK)
                at = b + lows[j]
                rows = pl.ds(at * BLOCK, BLOCK)
                mods = mods_ref[at : at + 1, :]
                branch = dot(mixes[j][source, :], mixer_w[...]) + as_row(mixer_b)
                middle = xs[j][source, :].astype(F32) + mods[:, cut(2)] * branch
                normed_mid = layer_norm(middle)[0] * (1.0 + mods[:, cut(4)]) + mods[:, cut(3)]
                normed_mid = normed_mid.astype(BF16)
                output_grad = (mods[:, cut(5)] * cotangent(at)).astype(BF16)
                branch_scr[rows, :] = branch
                middle_scr[rows, :] = middle
                normed_scr[rows, :] = normed_mid
                grad_scr[rows, :] = output_grad
                normed_t[:, rows] = normed_mid.T
                grad_t[:, rows] = output_grad.T
                ob_acc[...] += column_sum(output_grad.astype(F32))

    units_of = pl.ds(pl.multiple_of(f * part, part), part)

    @pl.loop(0, total // STEP)
    def _(m):
        rows = pl.ds(pl.multiple_of(m * STEP * BLOCK, STEP * BLOCK), STEP * BLOCK)
        hidden = dot(normed_scr[rows, :], hidden_w[...]) + as_row(hidden_b)
        square = hidden * hidden
        bend = 0.7978845608028654 * 0.044715
        curve = jnp.tanh(hidden * (0.7978845608028654 + bend * square))
        half = 0.5 + 0.5 * curve
        active = (hidden * half).astype(BF16)
        slope = half + (0.5 * hidden) * (1.0 - curve * curve) * (
            0.7978845608028654 + 3.0 * bend * square
        )
        hidden_grad = (dot_nt(grad_scr[rows, :], output_w[...]) * slope).astype(BF16)
        out_acc[rows, :] += dot(active, output_w[...])
        mid_acc[rows, :] += dot_nt(hidden_grad, hidden_w[...])
        ow_acc[:, units_of] += dot(grad_t[:, rows], active)
        hw_acc[:, units_of] += dot(normed_t[:, rows], hidden_grad)
        hb_acc[:, units_of] += column_sum(hidden_grad.astype(F32))

    @pl.when(f == SPLIT - 1)
    def _():
        for j in range(u):

            for b in range(units[j][1]):
                source = pl.ds(b * BLOCK, BLOCK)
                at = b + lows[j]
                rows = pl.ds(at * BLOCK, BLOCK)
                mods = mods_ref[at : at + 1, :]
                gate_one, scale_two, gate_two = mods[:, cut(2)], mods[:, cut(4)], mods[:, cut(5)]
                middle, branch = middle_scr[rows, :], branch_scr[rows, :]
                cot = cotangent(at)
                output = out_acc[rows, :] + as_row(output_b)
                result = (middle + gate_two * output).astype(BF16)
                for s in range(n):
                    out_ref[s, at] = result[s * chunk : (s + 1) * chunk]
                normed, inverse = layer_norm(middle)
                mid_grad = mid_acc[rows, :]
                middle_grad = cot + norm_back(mid_grad * (1.0 + scale_two), normed, inverse)
                middle_out[rows, :] = middle_grad
                branch_grad = (gate_one * middle_grad).astype(BF16)
                mw_acc[...] += dot(mixes[j][source, :].T, branch_grad)
                mb_acc[...] += column_sum(branch_grad.astype(F32))
                mixed_grad_out[rows, :] = dot_nt(branch_grad, mixer_w[...]).astype(BF16)
                found = (
                    column_sum(middle_grad * branch),
                    column_sum(mid_grad),
                    column_sum(mid_grad * normed),
                    column_sum(cot * output),
                )
                for m, row in enumerate(found):
                    slots_acc[m, at : at + 1, :] = row

        ff = ow_acc.shape[1]
        rows_scr[:ff, :] = ow_acc[...].T.astype(BF16)
        for j in range(ff // width):
            lo = ff + j * width
            rows_scr[lo : lo + width, :] = hw_acc[:, j * width : (j + 1) * width].astype(BF16)
        if rows_scr.shape[0] > 2 * ff:
            rows_scr[2 * ff :, :] = jnp.zeros((rows_scr.shape[0] - 2 * ff, width), BF16)
        spread_out(me_ref, rows_scr.shape[0] // size, size, rows_scr, (first_out, second_out))
        mixer_out[...] = mw_acc[...]
        sums = [ob_acc[...]]
        sums += [hb_acc[:, j * width : (j + 1) * width] for j in range(ff // width)]
        sums += [mb_acc[...], jnp.zeros((8 - 2 - ff // width, width), F32)]
        small = [slots_acc[m] for m in range(4)] + [activity_ref[...]] + sums
        small_out[...] = jnp.concatenate(small, axis=0).astype(BF16)


def feed(units, n, chunk, size, me, valid, xs, mixes, cots, mods, activity, weights):
    width, ff = weights[2].shape
    total = sum(count for _, count in units)
    shape = jax.ShapeDtypeStruct
    tokens, part = total * BLOCK, ff // SPLIT
    arrays = [*xs, *mixes, cots, mods, activity, *weights]
    in_specs = [full(a.shape) for a in arrays]
    in_specs[-4] = pl.BlockSpec((width, part), lambda f: (0, f))
    in_specs[-3] = pl.BlockSpec((part,), lambda f: (f,))
    in_specs[-2] = pl.BlockSpec((part, width), lambda f: (f, 0))
    rows = padded(2 * ff, size)
    outs = [shape((n, total, chunk, width), BF16)]
    outs += [shape((tokens, width), F32), shape((tokens, width), BF16)]
    outs += [shape((rows // 2, width), BF16)] * 2
    outs += [shape((width, width), F32), shape((48, width), BF16)]
    in_specs, arrays = [SMEM] + in_specs, [me] + arrays
    if valid is not None:
        in_specs, arrays = [SMEM] + in_specs, [me, valid] + arrays[1:]
    found = pl.pallas_call(
        partial(feed_kernel, units, n, chunk, width, size, valid is not None),
        grid=(SPLIT,),
        in_specs=in_specs,
        out_specs=[full(o.shape) for o in outs],
        out_shape=outs,
        scratch_shapes=[
            pltpu.VMEM((tokens, width), F32),
            pltpu.VMEM((tokens, width), F32),
            pltpu.VMEM((tokens, width), F32),
            pltpu.VMEM((tokens, width), F32),
            pltpu.VMEM((tokens, width), BF16),
            pltpu.VMEM((tokens, width), BF16),
            pltpu.VMEM((width, tokens), BF16),
            pltpu.VMEM((width, tokens), BF16),
            pltpu.VMEM((width, ff), F32),
            pltpu.VMEM((width, ff), F32),
            pltpu.VMEM((width, width), F32),
            pltpu.VMEM((1, width), F32),
            pltpu.VMEM((1, ff), F32),
            pltpu.VMEM((1, width), F32),
            pltpu.VMEM((rows, width), BF16),
            pltpu.VMEM((4, 8, width), F32),
        ],
        compiler_params=params(),
        cost_estimate=cost(0.1),
        name="feed",
    )(*arrays)
    return found[0], found[1:]


def finish_kernel(units, n, chunk, width, count, *refs):
    u = len(units)
    total = sum(c for _, c in units)
    xs, refs = refs[:u], refs[u:]
    parts, weight_ref, refs = refs[: 3 * PAIRS], refs[3 * PAIRS], refs[3 * PAIRS + 1 :]
    if u > 1:
        own_ref, others, refs = refs[0], refs[1 : 1 + count], refs[1 + count :]
    sums, refs = refs[0], refs[1:]
    middle_ref, mods_ref, out_ref, small_out, x_scr, g_scr, slots_acc = refs
    i = pl.program_id(0)

    @pl.when(i == 0)
    def _():
        slots_acc[...] = jnp.zeros_like(slots_acc)

    @pl.when(i < HALF)
    def _():
        x_scr[...] = xs[0][...]
        grads = jnp.concatenate([part[0] for part in parts], axis=1)
        g_scr[...] = dot_nt(grads, weight_ref[...])

    if u > 1:

        @pl.when(i >= HALF)
        def _():
            x_scr[...] = xs[1][...]
            grad = own_ref[...]
            for other in others:
                grad = grad + other[...].astype(F32)
            g_scr[...] = grad

    scale_one = mods_ref[pl.ds(i, 1), width : 2 * width]
    normed, inverse = layer_norm(x_scr[...].astype(F32))
    grad = g_scr[...]
    slots_acc[0, pl.ds(i, 1), :] = column_sum(grad)
    slots_acc[1, pl.ds(i, 1), :] = column_sum(grad * normed)
    result = middle_ref[...] + norm_back(grad * (1.0 + scale_one), normed, inverse)
    result = result.astype(BF16)
    for s in range(n):
        out_ref[s, 0] = result[s * chunk : (s + 1) * chunk]

    @pl.when(i == total - 1)
    def _():
        biases = [
            jnp.concatenate(
                [sums[j, 0:1, m * LANES : (m + 1) * LANES] for j in range(PAIRS)], axis=1
            )
            for m in (0, 2)
        ]
        small = [slots_acc[0], slots_acc[1], *biases, jnp.zeros((14, width), F32)]
        small_out[...] = jnp.concatenate(small, axis=0).astype(BF16)


def finish(units, n, chunk, xs, parts, weight, own, others, sums, middle, mods):
    width = middle.shape[1]
    total = sum(count for _, count in units)
    shape = jax.ShapeDtypeStruct
    lows = [sum(count for _, count in units[:j]) for j in range(len(units))]

    def rows_of(j, columns):
        return pl.BlockSpec(
            (BLOCK, columns), lambda i: (jnp.clip(i - lows[j], 0, units[j][1] - 1), 0)
        )

    in_specs = [rows_of(j, width) for j in range(len(units))]
    arrays = list(xs)
    for part in parts:
        for p in range(PAIRS):
            in_specs.append(
                pl.BlockSpec(
                    (1, BLOCK, LANES), lambda i, p=p: (p, jnp.clip(i, 0, HALF - 1), 0)
                )
            )
            arrays.append(part)
    in_specs.append(full(weight.shape))
    arrays.append(weight)
    if len(units) > 1:
        in_specs += [rows_of(1, width)] * (1 + len(others))
        arrays += [own, *others]
    in_specs += [full(sums.shape)]
    in_specs += [pl.BlockSpec((BLOCK, width), lambda i: (i, 0)), full(mods.shape)]
    arrays += [sums, middle, mods]
    return pl.pallas_call(
        partial(finish_kernel, units, n, chunk, width, len(others)),
        grid=(total,),
        in_specs=in_specs,
        out_specs=[
            pl.BlockSpec((n, 1, chunk, width), lambda i: (0, i, 0, 0)),
            full((32, width)),
        ],
        out_shape=[shape((n, total, chunk, width), BF16), shape((32, width), BF16)],
        scratch_shapes=[
            pltpu.VMEM((BLOCK, width), BF16),
            pltpu.VMEM((BLOCK, width), F32),
            pltpu.VMEM((2, 8, width), F32),
        ],
        compiler_params=params(),
        cost_estimate=cost(0.1),
        name="finish",
    )(*arrays)


def settle_kernel(size, chunk, places, kept, me_ref, *refs):
    pieces, outs, small_out, rows_scr = refs[:kept], refs[kept:-2], refs[-2], refs[-1]
    held = pieces[0].shape[0] // (size // kept)
    for j, piece in enumerate(pieces):

        @pl.loop(0, size // kept)
        def _(p, j=j, piece=piece):
            at = pl.multiple_of(((p + j * (size // kept)) ^ me_ref[0]) * chunk, chunk)
            low = pl.multiple_of(p * held, 16)
            rows_scr[pl.ds(at, chunk), :] = piece[pl.ds(low, chunk), :].astype(F32)
            small_out[p + j * (size // kept)] = piece[pl.ds(low + chunk, held - chunk), :].astype(F32)

    width = rows_scr.shape[1]
    for out, low in zip(outs, places):
        rows = out.shape[0]
        for c in range(out.shape[1] // width):
            out[:, c * width : (c + 1) * width] = rows_scr[low + c * rows : low + (c + 1) * rows, :]


def settle(size, chunk, me, pieces, shapes):
    width = pieces[0].shape[1]
    held = pieces[0].shape[0] * len(pieces) // size
    places, low = [], 0
    for rows, columns in shapes:
        places.append(low)
        low += rows * (columns // width)
    shapes = [*shapes, (size, held - chunk, width)]
    return pl.pallas_call(
        partial(settle_kernel, size, chunk, places, len(pieces)),
        in_specs=[SMEM] + [full(h.shape) for h in pieces],
        out_specs=[full(s) for s in shapes],
        out_shape=[jax.ShapeDtypeStruct(s, F32) for s in shapes],
        grid=(1,),
        scratch_shapes=[pltpu.VMEM((size * chunk, width), F32)],
        compiler_params=params(40),
        cost_estimate=cost(0.1),
        name="settle",
    )(me, *pieces)


def modulate_kernel(early_ref, late_ref, weight_out, bias_out, query_out, value_out, *outs):
    size, _, width = early_ref.shape
    mixer_out, hidden_out, output_out = outs
    flat = lambda ref, m: ref[:, 8 * m : 8 * (m + 1), :].reshape(size * 8, width)
    activity = flat(early_ref, 4).astype(BF16).T
    for m in range(6):
        slots = flat(late_ref, m) if m < 2 else flat(early_ref, m - 2)
        lanes = slice(m * width, (m + 1) * width)
        weight_out[:, lanes] = dot(activity, slots.astype(BF16))
        bias_out[lanes] = column_sum(slots).reshape(-1)
    early = jnp.sum(early_ref[:, 40:48, :], axis=0)
    late = jnp.sum(late_ref[:, 16:24, :], axis=0)
    query_out[...] = late[0:1].reshape(-1)
    value_out[...] = late[1:2].reshape(-1)
    output_out[...] = early[0:1].reshape(-1)
    parts = hidden_out.shape[0] // width
    for j in range(parts):
        hidden_out[j * width : (j + 1) * width] = early[1 + j : 2 + j].reshape(-1)
    mixer_out[...] = early[1 + parts : 2 + parts].reshape(-1)


def modulate(early, late, ff):
    width = early.shape[2]
    shapes = [(width, 6 * width), (6 * width,), (width,), (width,), (width,), (ff,), (width,)]
    return pl.pallas_call(
        modulate_kernel,
        out_shape=[jax.ShapeDtypeStruct(s, F32) for s in shapes],
        compiler_params=params(40),
        cost_estimate=cost(0.1),
        name="modulate",
    )(early, late)


def xor_permute(value, mask, size):
    return lax.ppermute(value, ("rows", "band"), [(i, i ^ mask) for i in range(size)])


def stages_of(rows, bands):
    band_bits, bits = bands.bit_length() - 1, (rows * bands).bit_length() - 1
    stages = [[band_bits]]
    for low, high in ((band_bits + 1, bits), (0, band_bits)):
        if (high - low) % 2:
            stages.append([low])
            low += 1
        stages += [[b, b + 1] for b in range(low, high, 2)]
    return stages


def digit_of(me, stage):
    return sum(((me >> b) & 1) << i for i, b in enumerate(stage))


def mask_of(t, stage):
    return sum(((t >> i) & 1) << b for i, b in enumerate(stage))


def fold_kernel(count, *refs):
    total = refs[0][...].astype(F32)
    for ref in refs[1:count]:
        total = total + ref[...].astype(F32)
    outs = refs[count:]
    rows = total.shape[0] // len(outs)
    for j, out in enumerate(outs):
        out[...] = total[j * rows : (j + 1) * rows].astype(BF16)


def fold(arrays, parts):
    rows, width = arrays[0].shape
    shape = jax.ShapeDtypeStruct((rows // parts, width), BF16)
    found = pl.pallas_call(
        partial(fold_kernel, len(arrays)),
        out_shape=[shape] * parts,
        compiler_params=params(32),
        cost_estimate=cost(0.1),
        name="fold",
    )(*arrays)
    return list(found)


def after(value, *others):
    return lax.optimization_barrier((value, others))[0]


def join_kernel(count, *refs):
    rows = refs[0].shape[0]
    for j in range(count):
        refs[count][j * rows : (j + 1) * rows, :] = refs[j][...]


def join(arrays):
    rows, width = arrays[0].shape
    return pl.pallas_call(
        partial(join_kernel, len(arrays)),
        out_shape=jax.ShapeDtypeStruct((rows * len(arrays), width), BF16),
        compiler_params=params(32),
        cost_estimate=cost(0.1),
        name="join",
    )(*arrays)


class Sum:
    def __init__(self, stages, size, parts):
        self.stages, self.size, self.at = stages, size, 0
        self.scattered = False
        self.steps = self.left = 2 * len(stages) - 1
        self.send(parts)

    def send(self, parts):
        stage = self.stages[self.at]
        self.held = [parts[0]] + [
            xor_permute(part, mask_of(t, stage), self.size) for t, part in enumerate(parts) if t
        ]

    def step(self, extra=None, done=()):
        held = list(after(self.held, *done)) if done else self.held
        self.left -= 1
        self.at += -1 if self.scattered else 1
        if not self.scattered and self.at < len(self.stages):
            parts = fold(held, 1 << len(self.stages[self.at]))
            self.send(parts)
            return parts
        if not self.scattered:
            self.scattered = True
            self.at -= 1
            value = fold(held, 1)[0]
            if extra is not None:
                value = jnp.concatenate([value, extra], axis=0)
        else:
            value = join(held)
        self.send([value] * (1 << len(self.stages[self.at])))
        return [value]


def body(
    patches,
    condition_table,
    condition_index,
    image_lengths,
    modulate_weight,
    modulate_bias,
    triple_weight,
    query_bias,
    value_bias,
    mixer_weight,
    mixer_bias,
    hidden_weight,
    hidden_bias,
    output_weight,
    output_bias,
    cotangent,
):
    band = lax.axis_index("band")
    n = lax.axis_size("band")
    size = n * lax.axis_size("rows")
    everyone = lax.axis_index(("rows", "band"))
    rows, band_length, width = patches.shape
    ff = hidden_weight.shape[1]
    length = band_length * n
    big = length // 2
    chunk = band_length // (2 * HALF)
    assert length == 2 * HALF * BLOCK
    plan = Plan(rows, n)
    units, total = plan.units(), plan.total
    assert units[0][1] == HALF
    stages = stages_of(size // n, n)
    relative = jnp.int32(0)
    for stage in stages:
        relative = (relative << len(stage)) | digit_of(everyone, stage)
    relative = relative.astype(jnp.int32).reshape(1)

    def deal(pieces):
        return lax.all_to_all(pieces, "band", 0, 0, tiled=True)

    me = band.astype(jnp.int32).reshape(1)
    packed = pack(plan, chunk, big, me, image_lengths, patches, True)
    x_pieces = [p if s == 0 else xor_permute(p, s, size) for s, p in enumerate(packed)]

    mods, activity, flags = prepare(
        plan,
        big,
        me,
        image_lengths,
        condition_index,
        condition_table,
        modulate_weight,
        modulate_bias,
    )
    c_packed = pack(plan, chunk, big, me, image_lengths, after(cotangent, packed), False)
    c_pieces = deal(after(c_packed, mods, x_pieces[1:TIE]))

    attended, xs, mixes = [], [], []
    others = [[] for _ in units]
    if plan.group > 1:
        own = collect(n, plan.whole * HALF, plan.own, chunk, me, x_pieces)
        others[-1] = [xor_permute(own, t, size) for t in range(1, plan.group)]
    for j, (name, count) in enumerate(units):
        lo = j * HALF
        found = attend(
            n,
            j,
            lo,
            count,
            HALF,
            chunk,
            me,
            flags,
            x_pieces,
            others[j],
            mods,
            triple_weight,
            query_bias,
            value_bias,
        )
        xs.append(found[0])
        attended.append(found[1:8])
        mixes.append(found[8])

    valid = None
    if plan.idle:
        valid = (plan.half_row("shared", band) < plan.halves).astype(F32).reshape(1)

    weights = [
        mixer_weight,
        mixer_bias,
        hidden_weight,
        hidden_bias,
        output_weight,
        output_bias,
    ]
    out_pieces, fed = feed(
        units,
        n,
        chunk,
        size,
        relative,
        valid,
        xs,
        mixes,
        c_pieces,
        mods,
        activity,
        weights,
    )
    middle_grad, mixed_grad, first, second, mixer_grad, feed_small = fed
    out_back = deal(out_pieces)
    feed_sum = Sum(stages, size, [first, second])

    own, others, begun = None, [], []
    token = feed_sum.step()
    mixed_grad = after(mixed_grad, *token)
    if len(units) > 1:
        kept, low = attended[1], HALF
        found = shared_back(units[1][1], HALF, flags, kept, mixed_grad, low, triple_weight)
        own, others = found[0], [xor_permute(o, t + 1, size) for t, o in enumerate(found[1:-2])]
        begun = found[-2:]
        token = feed_sum.step(feed_small, done=(own,))
    grad = after(mixed_grad, *token)
    *parts, sums, first, second = whole_back(
        size, relative, flags, attended[0], grad, begun, mixer_grad
    )
    token = feed_sum.step(feed_small, done=(sums,))
    grad_pieces, last_small = finish(
        units,
        n,
        chunk,
        xs,
        parts,
        triple_weight,
        own,
        others,
        sums,
        after(middle_grad, out_back, *token),
        mods,
    )
    feed_chunk, last_chunk = (padded(r, size) // size for r in (2 * ff, 4 * width))
    last_sum = Sum(stages, size, after([first, second], last_small))
    spreading = feed_sum.step(feed_small, done=(last_small,))
    grad_back = deal(after(grad_pieces, spreading))
    last_sum.step(last_small)
    last_sum.step(last_small)
    token = last_sum.step(last_small)
    feed_sum.step(feed_small, done=token)
    token = last_sum.step(last_small, done=(grad_back,))
    while feed_sum.left:
        feed_sum.step(feed_small, done=token)
        token = last_sum.step(last_small)
    block_out = unpack(plan, chunk, big, image_lengths, out_back, BF16)
    output_w_grad, hidden_w_grad, early = settle(
        size, feed_chunk, relative, feed_sum.held, [(ff, width), (width, ff)]
    )
    patch_grad = unpack(plan, chunk, big, image_lengths, grad_back, F32)
    while last_sum.left:
        token = ()
        if last_sum.left == 1:
            token = (patch_grad, block_out, output_w_grad)
        last_sum.step(last_small, done=token)
    triple_w_grad, mixer_w_grad, late = settle(
        size, last_chunk, relative, last_sum.held, [(width, 3 * width), (width, width)]
    )
    modulate_w_grad, modulate_b_grad, query_b, value_b, mixer_b, hidden_b, output_b = modulate(
        early, late, ff
    )
    return (
        block_out,
        patch_grad,
        modulate_w_grad,
        modulate_b_grad,
        triple_w_grad,
        query_b,
        value_b,
        mixer_w_grad,
        mixer_b,
        hidden_w_grad,
        hidden_b,
        output_w_grad,
        output_b,
    )


def solution(mesh):
    return jax.shard_map(
        body,
        mesh=mesh,
        in_specs=(
            P("rows", None, "band"),
            P(),
            P("rows", None),
            P("rows", None),
            P(),
            P(),
            P(),
            P(),
            P(),
            P(),
            P(),
            P(),
            P(),
            P(),
            P(),
            P("rows", None, "band"),
        ),
        out_specs=(
            P("rows", None, "band"),
            P("rows", None, "band"),
            P(),
            P(),
            P(),
            P(),
            P(),
            P(),
            P(),
            P(),
            P(),
            P(),
            P(),
        ),
        check_vma=False,
    )
```

```python
from functools import partial

import jax
import jax.numpy as jnp
from jax import lax
from jax.experimental import pallas as pl
from jax.experimental.pallas import tpu as pltpu
from jax.sharding import PartitionSpec as P

HEADS = 6
HEAD_DIM = 64
PAIRS = HEADS // 2
LANES = 128
BLOCK = 256
HALF = 4
EPSILON = 1e-06
ONES = 16
TIE = 8
F32 = jnp.float32
BF16 = jnp.bfloat16
MIB = 1 << 20


def dot(left, right):
    return jnp.dot(left, right, preferred_element_type=F32)


def dot_nt(left, right):
    return lax.dot_general(left, right, (((1,), (1,)), ((), ())), preferred_element_type=F32)


def params(limit=56, **more):
    return pltpu.CompilerParams(vmem_limit_bytes=limit * MIB, **more)


def cost(micros):
    return pl.CostEstimate(flops=0, bytes_accessed=int(micros * 3e6), transcendentals=0)


def full(shape):
    return pl.BlockSpec(shape, lambda *_: (0,) * len(shape))


SMEM = pl.BlockSpec(memory_space=pltpu.SMEM)


def row_layout(lens_ref, row, slots, big):
    count = jnp.int32(0)
    before = jnp.int32(0)
    for j in range(slots):
        is_big = (lens_ref[row, j] == big).astype(jnp.int32)
        before = before + jnp.where(count + is_big == 0, 1, 0)
        count = count + is_big
    return count, jnp.where(count == 1, before, 0)


def chunk_of(start, half, k):
    return jnp.where(half == 0, start + k, jnp.where(k < start, k, k + HALF))


class Plan:
    def __init__(self, rows, bands):
        self.rows, self.bands = rows, bands
        self.halves = 2 * rows
        self.whole = self.halves // bands
        assert self.whole <= 1
        self.rest = self.halves - self.whole * bands
        self.group = 1
        while self.rest and self.rest * self.group * 2 <= bands and self.group < HALF:
            self.group *= 2
        self.idle = self.rest * self.group != bands
        self.own = HALF // self.group

    @property
    def total(self):
        return sum(count for _, count in self.units())

    def units(self):
        found = []
        if self.whole:
            found.append(("whole", HALF))
        if self.rest:
            found.append(("shared", self.own))
        return found

    def half_row(self, name, device):
        if name == "whole":
            return device
        return self.whole * self.bands + device // self.group

    def first(self, name, device):
        return 0 if name == "whole" else (device % self.group) * self.own


def pack_kernel(plan, chunk, slots, big, apart, me_ref, lens_ref, x_ref, *outs):
    for s in range(plan.bands):
        dest = me_ref[0] ^ s if apart else s
        at = 0
        for name, count in plan.units():
            half_row = jnp.minimum(plan.half_row(name, dest), plan.halves - 1)
            row, half = half_row // 2, half_row % 2
            start = row_layout(lens_ref, row, slots, big)[1]
            for k in range(count):
                source = chunk_of(start, half, plan.first(name, dest) + k)
                rows = pl.ds(pl.multiple_of(source * chunk, chunk), chunk)
                if apart:
                    outs[s][at] = x_ref[row, rows, :]
                else:
                    outs[0][dest, at] = x_ref[row, rows, :]
                at += 1


def pack(plan, chunk, big, me, lens, x, apart):
    shape = (plan.total, chunk, x.shape[2])
    shapes = [shape] * plan.bands if apart else [(plan.bands,) + shape]
    found = pl.pallas_call(
        partial(pack_kernel, plan, chunk, lens.shape[1], big, apart),
        in_specs=[SMEM, SMEM, full(x.shape)],
        out_specs=[full(s) for s in shapes],
        out_shape=[jax.ShapeDtypeStruct(s, x.dtype) for s in shapes],
        grid=(1,),
        compiler_params=params(32),
        cost_estimate=cost(0.1),
        name="pack",
    )(me, lens, x)
    return found if apart else found[0]


def unpack_kernel(plan, chunk, slots, big, lens_ref, piece_ref, out_ref):
    for owner in range(plan.bands):
        at = 0
        for name, count in plan.units():
            half_row = plan.half_row(name, owner)
            if half_row < plan.halves:
                row, half = half_row // 2, half_row % 2
                start = row_layout(lens_ref, row, slots, big)[1]
                for k in range(count):
                    source = chunk_of(start, half, plan.first(name, owner) + k)
                    rows = pl.ds(pl.multiple_of(source * chunk, chunk), chunk)
                    out_ref[row, rows, :] = piece_ref[owner, at + k].astype(out_ref.dtype)
            at += count


def unpack(plan, chunk, big, lens, pieces, dtype):
    shape = (plan.rows, chunk * 2 * HALF, pieces.shape[3])
    return pl.pallas_call(
        partial(unpack_kernel, plan, chunk, lens.shape[1], big),
        in_specs=[SMEM, full(pieces.shape)],
        out_specs=full(shape),
        out_shape=jax.ShapeDtypeStruct(shape, dtype),
        grid=(1,),
        compiler_params=params(32),
        cost_estimate=cost(0.1),
        name="unpack",
    )(lens, pieces)


def collect_kernel(n, low, count, chunk, me_ref, *refs):
    for b in range(count):
        for s in range(n):
            at = pl.multiple_of(b * BLOCK + (me_ref[0] ^ s) * chunk, chunk)
            refs[n][pl.ds(at, chunk), :] = refs[s][low + b]


def collect(n, low, count, chunk, me, pieces):
    width = pieces[0].shape[2]
    return pl.pallas_call(
        partial(collect_kernel, n, low, count, chunk),
        in_specs=[SMEM] + [full(p.shape) for p in pieces],
        out_specs=full((count * BLOCK, width)),
        out_shape=jax.ShapeDtypeStruct((count * BLOCK, width), BF16),
        grid=(1,),
        compiler_params=params(16),
        cost_estimate=cost(0.1),
        name="collect",
    )(me, *pieces)


def prepare_kernel(plan, slots, big, me_ref, lens_ref, index_ref, table_ref, weight_ref, bias_ref, *refs):
    mods_out, activity_out, flags_out, table_scr, activity_scr = refs
    table_scr[...] = table_ref[...].astype(F32)
    activity_scr[...] = jnp.zeros_like(activity_scr)
    at = 0
    for j, (name, count) in enumerate(plan.units()):
        half_row = jnp.minimum(plan.half_row(name, me_ref[0]), plan.halves - 1)
        row, half = half_row // 2, half_row % 2
        bigs, start = row_layout(lens_ref, row, slots, big)
        is_big = jnp.logical_or(bigs == 2, jnp.logical_and(bigs == 1, half == 0))
        flags_out[j] = is_big.astype(jnp.int32)
        for t in range(HALF // count):
            first = 0 if count == HALF else ((me_ref[0] % plan.group) ^ t) * count
            for k in range(count):
                place = first + k
                single = jnp.where(half == 0, start, jnp.where(place < start, place, place + 1))
                slot = jnp.where(bigs == 2, half, jnp.where(bigs == 0, HALF * half + place, single))
                chosen = table_scr[pl.ds(index_ref[row, slot], 1), :]
                activity_scr[at : at + 1, :] = chosen * (1.0 / (1.0 + jnp.exp(-chosen)))
                at += 1
    activity = activity_scr[...].astype(BF16)
    activity_out[...] = activity.astype(F32)
    mods_out[...] = dot(activity, weight_ref[...]) + as_row(bias_ref)


def prepare(plan, big, me, lens, index, table, weight, bias):
    width = table.shape[1]
    shape = jax.ShapeDtypeStruct
    arrays = [table, weight, bias]
    return pl.pallas_call(
        partial(prepare_kernel, plan, lens.shape[1], big),
        in_specs=[SMEM] * 3 + [full(a.shape) for a in arrays],
        out_specs=[full((8, weight.shape[1])), full((8, width)), SMEM],
        out_shape=[
            shape((8, weight.shape[1]), F32),
            shape((8, width), F32),
            shape((2,), jnp.int32),
        ],
        grid=(1,),
        scratch_shapes=[pltpu.VMEM(table.shape, F32), pltpu.VMEM((8, width), F32)],
        compiler_params=params(32),
        cost_estimate=cost(0.1),
        name="prepare",
    )(me, lens, index, *arrays)


def layer_norm(values):
    centre = values - jnp.mean(values, axis=-1, keepdims=True)
    inverse = lax.rsqrt(jnp.mean(centre * centre, axis=-1, keepdims=True) + EPSILON)
    return centre * inverse, inverse


def norm_back(grad, normed, inverse):
    return inverse * (
        grad
        - jnp.mean(grad, axis=-1, keepdims=True)
        - normed * jnp.mean(grad * normed, axis=-1, keepdims=True)
    )


def as_row(ref):
    return ref[...].astype(F32).reshape(1, -1)


def column_sum(values):
    return jnp.sum(values, axis=0, keepdims=True)


def attend_kernel(n, unit, low, nq, nk, chunk, width, me_ref, flag_ref, *refs):
    pieces, refs = refs[:n], refs[n:]
    count = nk // nq - 1
    others, refs = refs[:count], refs[count:]
    mods_ref, weight_ref, query_bias_ref, value_bias_ref = refs[:4]
    x_out, hint_out, q_out, k_out, v_out, e_out, ot_out, inv_out, mixed_out = refs[4:13]
    k_scr, qt_scr, vt_scr = refs[13:]
    p = pl.program_id(0)

    @pl.when(p == 0)
    def _():
        qt_scr[...] = jnp.zeros_like(qt_scr)
        for h in range(HEADS):
            vt_scr[h, HEAD_DIM:, :] = jnp.ones((ONES, nk * BLOCK), BF16)
        for b in range(nk):
            rows = pl.ds(b * BLOCK, BLOCK)
            if b < nq:
                for s in range(n):
                    at = pl.multiple_of(b * BLOCK + (me_ref[0] ^ s) * chunk, chunk)
                    x_out[pl.ds(at, chunk), :] = pieces[s][low + b]
            else:
                t, inner = b // nq - 1, b % nq
                x_out[rows, :] = others[t][pl.ds(inner * BLOCK, BLOCK), :]
            source = x_out[rows, :].astype(F32)
            normed = layer_norm(source)[0]
            shift = mods_ref[low + b : low + b + 1, 0:width]
            scale = mods_ref[low + b : low + b + 1, width : 2 * width]
            hin = (normed * (1.0 + scale) + shift).astype(BF16)
            hint_out[:, rows] = hin.T
            triple = dot(hin, weight_ref[...])
            keys = triple[:, width : 2 * width].astype(BF16)
            values = (triple[:, 2 * width :] + as_row(value_bias_ref)).astype(BF16)
            values_t = values.T
            for j in range(PAIRS):
                lanes = slice(j * LANES, (j + 1) * LANES)
                k_scr[j, rows, :] = keys[:, lanes]
                k_out[j, rows, :] = keys[:, lanes]
                v_out[j, rows, :] = values[:, lanes]
            for h in range(HEADS):
                vt_scr[h, :HEAD_DIM, rows] = values_t[h * HEAD_DIM : (h + 1) * HEAD_DIM]
            if b < nq:
                query = (triple[:, :width] + as_row(query_bias_ref)) * (HEAD_DIM**-0.5)
                query = query.astype(BF16)
                for j in range(PAIRS):
                    q_out[j, rows, :] = query[:, j * LANES : (j + 1) * LANES]
                query_t = query.T
                for h in range(HEADS):
                    to = (h % 2) * HEAD_DIM
                    qt_scr[h, to : to + HEAD_DIM, rows] = query_t[
                        h * HEAD_DIM : (h + 1) * HEAD_DIM
                    ]

    def tile(columns, krows):
        found = []
        for hh in range(2):
            h = 2 * p + hh
            scores = dot(k_scr[p, krows, :], qt_scr[h, :, columns])
            exps = jnp.exp(scores - jnp.max(scores, axis=0, keepdims=True)).astype(BF16)
            e_out[hh, krows, columns] = exps
            summed = dot(vt_scr[h, :, krows], exps)
            inverse = 1.0 / summed[HEAD_DIM : HEAD_DIM + 1]
            found.append(summed[:HEAD_DIM] * inverse)
            inv_out[0, hh : hh + 1, columns] = inverse
        both = jnp.concatenate(found, axis=0)
        ot_out[0, :, columns] = both
        mixed_out[columns, :] = both.T.astype(BF16)

    @pl.when(flag_ref[unit] == 1)
    def _():
        tile(pl.ds(0, nq * BLOCK), pl.ds(0, nk * BLOCK))

    @pl.when(flag_ref[unit] == 0)
    def _():
        for b in range(nq):
            tile(pl.ds(b * BLOCK, BLOCK), pl.ds(b * BLOCK, BLOCK))


def attend(n, unit, low, nq, nk, chunk, me, flag, pieces, others, mods, weight, query_bias, value_bias):
    width = weight.shape[0]
    qs, ks = nq * BLOCK, nk * BLOCK
    shape = jax.ShapeDtypeStruct
    outs = [
        (shape((ks, width), BF16), None),
        (shape((width, ks), BF16), None),
        (shape((PAIRS, qs, LANES), BF16), None),
        (shape((PAIRS, ks, LANES), BF16), None),
        (shape((PAIRS, ks, LANES), BF16), None),
        (shape((HEADS, ks, qs), BF16), pl.BlockSpec((2, ks, qs), lambda p: (p, 0, 0))),
        (shape((PAIRS, LANES, qs), F32), pl.BlockSpec((1, LANES, qs), lambda p: (p, 0, 0))),
        (shape((PAIRS, 8, qs), F32), pl.BlockSpec((1, 8, qs), lambda p: (p, 0, 0))),
        (shape((qs, width), BF16), pl.BlockSpec((qs, LANES), lambda p: (0, p))),
    ]
    arrays = [*pieces, *others, mods, weight, query_bias, value_bias]
    flops = 2 * ks * width * 3 * width + 4 * HEADS * qs * ks * HEAD_DIM * 4
    return pl.pallas_call(
        partial(attend_kernel, n, unit, low, nq, nk, chunk, width),
        grid=(PAIRS,),
        in_specs=[SMEM, SMEM] + [full(a.shape) for a in arrays],
        out_specs=[spec or full(s.shape) for s, spec in outs],
        out_shape=[s for s, _ in outs],
        scratch_shapes=[
            pltpu.VMEM((PAIRS, ks, LANES), BF16),
            pltpu.VMEM((HEADS, LANES, qs), BF16),
            pltpu.VMEM((HEADS, HEAD_DIM + ONES, ks), BF16),
        ],
        compiler_params=params(),
        cost_estimate=cost(0.1),
        name="attend",
    )(me, flag, *arrays)


def back_tile(qlow, qsize, klow, ksize, e_ref, q_ref, k_ref, v_ref, ot_ref, inv_ref, grad_ref):
    columns, krows = pl.ds(qlow, qsize), pl.ds(klow, ksize)
    lane = lax.broadcasted_iota(jnp.int32, (qsize, LANES), 1)
    grad_t = grad_ref[columns, :].astype(F32).T
    keys_t = k_ref[0, krows, :].T
    query = q_ref[0, columns, :]
    zeros = jnp.zeros((HEAD_DIM, qsize), BF16)
    found, keys_grad, values_grad = [], None, None
    for hh in range(2):
        part = slice(hh * HEAD_DIM, (hh + 1) * HEAD_DIM)
        scaled = (grad_t[part] * inv_ref[0, hh : hh + 1, columns]).astype(BF16)
        delta = column_sum(scaled.astype(F32) * ot_ref[0, part, columns])
        masked = jnp.concatenate([scaled, zeros] if hh == 0 else [zeros, scaled], axis=0)
        exps = e_ref[hh, krows, columns]
        prob_grad = dot(v_ref[0, krows, :], masked)
        score_grad = (exps.astype(F32) * (prob_grad - delta)).astype(BF16)
        own = (lane < HEAD_DIM) if hh == 0 else (lane >= HEAD_DIM)
        values_part = dot_nt(exps, masked)
        keys_part = dot(score_grad, jnp.where(own, query, jnp.zeros_like(query)))
        values_grad = values_part if hh == 0 else values_grad + values_part
        keys_grad = keys_part if hh == 0 else keys_grad + keys_part
        found.append(dot(keys_t[part], score_grad))
    both = jnp.concatenate(found, axis=0) * (HEAD_DIM**-0.5)
    return both.T.astype(BF16), keys_grad.astype(BF16), values_grad.astype(BF16)


def shared_back_kernel(nq, nk, flag_ref, *refs):
    tile_refs, (hint_ref, weight_ref, own_out), refs = refs[:7], refs[7:10], refs[10:]
    others_out, (tw_out, tb_out, tg_scr) = refs[:-3], refs[-3:]
    p = pl.program_id(0)
    qs, rest = nq * BLOCK, (nk - nq) * BLOCK

    def tile(qlow, qsize, klow, ksize):
        query_grad, keys_grad, values_grad = back_tile(qlow, qsize, klow, ksize, *tile_refs)
        tg_scr[p, pl.ds(qlow, qsize), :] = query_grad
        tg_scr[PAIRS + p, pl.ds(klow, ksize), :] = keys_grad
        tg_scr[2 * PAIRS + p, pl.ds(klow, ksize), :] = values_grad

    tg_scr[p, qs:, :] = jnp.zeros((rest, LANES), BF16)

    @pl.when(flag_ref[1] == 1)
    def _():
        tile(0, qs, 0, nk * BLOCK)

    @pl.when(flag_ref[1] == 0)
    def _():
        for j in (1, 2):
            tg_scr[j * PAIRS + p, qs:, :] = jnp.zeros((rest, LANES), BF16)
        for b in range(nq):
            tile(b * BLOCK, BLOCK, b * BLOCK, BLOCK)

    @pl.when(p == PAIRS - 1)
    def _():
        grads = jnp.concatenate([tg_scr[j] for j in range(3 * PAIRS)], axis=1)
        back = dot_nt(grads, weight_ref[...])
        own_out[...] = back[:qs]
        for t, out in enumerate(others_out):
            out[...] = back[(t + 1) * qs : (t + 2) * qs].astype(BF16)
        weight_grad = dot(hint_ref[...], grads)
        sums = column_sum(grads.astype(F32))
        for j in range(PAIRS):
            for m in range(3):
                low = (m * PAIRS + j) * LANES
                tw_out[j, :, m * LANES : (m + 1) * LANES] = weight_grad[:, low : low + LANES]
                tb_out[j, :, m * LANES : (m + 1) * LANES] = jnp.broadcast_to(
                    sums[:, low : low + LANES], (8, LANES)
                )


def whole_back_kernel(size, begun, flag_ref, *refs):
    tile_refs, hint_ref, refs = refs[:7], refs[7], refs[8:]
    if begun:
        tw_ref, tb_ref, refs = refs[0], refs[1], refs[2:]
    me_ref, mixer_ref, tq_out, tk_out, tv_out, tb_out, first_out, second_out, rows_scr = refs
    p = pl.program_id(0)

    def tile(qlow, qsize, klow, ksize):
        query_grad, keys_grad, values_grad = back_tile(qlow, qsize, klow, ksize, *tile_refs)
        tq_out[0, pl.ds(qlow, qsize), :] = query_grad
        tk_out[0, pl.ds(klow, ksize), :] = keys_grad
        tv_out[0, pl.ds(klow, ksize), :] = values_grad

    @pl.when(flag_ref[0] == 1)
    def _():
        tile(0, HALF * BLOCK, 0, HALF * BLOCK)

    @pl.when(flag_ref[0] == 0)
    def _():
        for b in range(HALF):
            tile(b * BLOCK, BLOCK, b * BLOCK, BLOCK)

    grads = jnp.concatenate([tq_out[0], tk_out[0], tv_out[0]], axis=1)
    weight_grad = dot(hint_ref[...], grads)
    sums = column_sum(grads.astype(F32))
    if begun:
        weight_grad, sums = weight_grad + tw_ref[0], sums + tb_ref[0, 0:1]
    tb_out[0] = jnp.broadcast_to(sums, tb_out.shape[1:])
    width = weight_grad.shape[0]
    lanes = pl.ds(pl.multiple_of(p * LANES, LANES), LANES)
    for m in range(3):
        rows_scr[m * width : (m + 1) * width, lanes] = weight_grad[
            :, m * LANES : (m + 1) * LANES
        ].astype(BF16)

    @pl.when(p == PAIRS - 1)
    def _():
        rows_scr[3 * width : 4 * width, :] = mixer_ref[...].astype(BF16)
        if rows_scr.shape[0] > 4 * width:
            rows_scr[4 * width :, :] = jnp.zeros((rows_scr.shape[0] - 4 * width, width), BF16)
        spread_out(me_ref, rows_scr.shape[0] // size, size, rows_scr, (first_out, second_out))


def back_inputs(nq, nk, first, flag, kept, grad, low):
    hint, q, k, v, e, ot, inv = kept
    qs, ks = nq * BLOCK, nk * BLOCK
    by_pair = lambda *tail: pl.BlockSpec((1,) + tail, lambda p: (first + p, 0, 0))
    in_specs = [
        SMEM,
        pl.BlockSpec((2, ks, qs), lambda p: (first + p, 0, 0)),
        by_pair(qs, LANES),
        by_pair(ks, LANES),
        by_pair(ks, LANES),
        by_pair(LANES, qs),
        by_pair(8, qs),
        pl.BlockSpec((qs, LANES), lambda p: (low * BLOCK // qs, first + p)),
        full(hint.shape),
    ]
    return in_specs, [flag, e, q, k, v, ot, inv, grad, hint]


def back_cost(qs, ks, steps):
    flops = 8 * 2 * steps * qs * ks * HEAD_DIM * 4
    return pl.CostEstimate(flops=flops, bytes_accessed=4 * steps * qs * ks, transcendentals=0)


def shared_back(nq, nk, flag, kept, grad, low, weight):
    width = weight.shape[0]
    qs, ks = nq * BLOCK, nk * BLOCK
    in_specs, arrays = back_inputs(nq, nk, 0, flag, kept, grad, low)
    shape = jax.ShapeDtypeStruct
    outs = [shape((qs, width), F32)] + [shape((qs, width), BF16)] * (nk // nq - 1)
    outs += [shape((PAIRS, width, 3 * LANES), F32), shape((PAIRS, 8, 3 * LANES), F32)]
    return pl.pallas_call(
        partial(shared_back_kernel, nq, nk),
        grid=(PAIRS,),
        in_specs=in_specs + [full(weight.shape)],
        out_specs=[full(o.shape) for o in outs],
        out_shape=outs,
        scratch_shapes=[pltpu.VMEM((3 * PAIRS, ks, LANES), BF16)],
        compiler_params=params(),
        cost_estimate=cost(0.1),
        name="shared_back",
    )(*arrays, weight)


def whole_back(size, me, flag, kept, grad, begun, mixer):
    width = mixer.shape[0]
    rows = HALF * BLOCK
    in_specs, arrays = back_inputs(HALF, HALF, 0, flag, kept, grad, 0)
    shape = jax.ShapeDtypeStruct
    if begun:
        in_specs += [pl.BlockSpec((1,) + b.shape[1:], lambda p: (p, 0, 0)) for b in begun]
        arrays += begun
    in_specs += [SMEM, full(mixer.shape)]
    arrays += [me, mixer]
    total = padded(4 * width, size)
    pairs = [shape((PAIRS, rows, LANES), BF16)] * 3 + [shape((PAIRS, 8, 3 * LANES), F32)]
    outs = pairs + [shape((total // 2, width), BF16)] * 2
    out_specs = [pl.BlockSpec((1,) + o.shape[1:], lambda p: (p, 0, 0)) for o in pairs]
    return pl.pallas_call(
        partial(whole_back_kernel, size, bool(begun)),
        grid=(PAIRS,),
        in_specs=in_specs,
        out_specs=out_specs + [full(o.shape) for o in outs[4:]],
        out_shape=outs,
        scratch_shapes=[pltpu.VMEM((total, width), BF16)],
        compiler_params=params(),
        cost_estimate=cost(0.1),
        name="whole_back",
    )(*arrays)


def spread_out(me_ref, chunk, size, source, outs):
    half = size // 2
    for j, out in enumerate(outs):

        @pl.loop(0, half)
        def _(p, j=j, out=out):
            at = pl.multiple_of(((p + j * half) ^ me_ref[0]) * chunk, chunk)
            out[pl.ds(pl.multiple_of(p * chunk, chunk), chunk), :] = source[pl.ds(at, chunk), :]


def padded(rows, size):
    return rows + -rows % (16 * size)


STEP = 6
SPLIT = 1


def feed_kernel(units, n, chunk, width, size, masked, me_ref, *refs):
    total = sum(count for _, count in units)
    u = len(units)
    if masked:
        valid_ref, refs = refs[0], refs[1:]
    xs, mixes, cot_ref, refs = refs[:u], refs[u : 2 * u], refs[2 * u], refs[2 * u + 1 :]
    mods_ref, activity_ref, mixer_w, mixer_b, hidden_w, hidden_b, output_w, output_b = refs[:8]
    out_ref, refs = refs[8], refs[9:]
    middle_out, mixed_grad_out, first_out, second_out, mixer_out, small_out, refs = *refs[:6], refs[6:]
    middle_scr, branch_scr, out_acc, mid_acc, normed_scr, grad_scr, normed_t, grad_t = refs[:8]
    ow_acc, hw_acc, mw_acc, ob_acc, hb_acc, mb_acc, rows_scr, slots_acc = refs[8:]
    f = pl.program_id(0)
    part = ow_acc.shape[1] // SPLIT
    cut = lambda at: slice(at * width, (at + 1) * width)
    lows = [sum(count for _, count in units[:j]) for j in range(u)]

    def cotangent(b):
        cot = jnp.concatenate([cot_ref[s, b] for s in range(n)], axis=0).astype(F32)
        return cot * valid_ref[0] if masked else cot

    @pl.when(f == 0)
    def _():
        for acc in (out_acc, mid_acc, ow_acc, hw_acc, mw_acc, ob_acc, hb_acc, mb_acc, slots_acc):
            acc[...] = jnp.zeros_like(acc)
        for j in range(u):

            for b in range(units[j][1]):
                source = pl.ds(b * BLOCK, BLOCK)
                at = b + lows[j]
                rows = pl.ds(at * BLOCK, BLOCK)
                mods = mods_ref[at : at + 1, :]
                branch = dot(mixes[j][source, :], mixer_w[...]) + as_row(mixer_b)
                middle = xs[j][source, :].astype(F32) + mods[:, cut(2)] * branch
                normed_mid = layer_norm(middle)[0] * (1.0 + mods[:, cut(4)]) + mods[:, cut(3)]
                normed_mid = normed_mid.astype(BF16)
                output_grad = (mods[:, cut(5)] * cotangent(at)).astype(BF16)
                branch_scr[rows, :] = branch
                middle_scr[rows, :] = middle
                normed_scr[rows, :] = normed_mid
                grad_scr[rows, :] = output_grad
                normed_t[:, rows] = normed_mid.T
                grad_t[:, rows] = output_grad.T
                ob_acc[...] += column_sum(output_grad.astype(F32))

    units_of = pl.ds(pl.multiple_of(f * part, part), part)

    @pl.loop(0, total // STEP)
    def _(m):
        rows = pl.ds(pl.multiple_of(m * STEP * BLOCK, STEP * BLOCK), STEP * BLOCK)
        hidden = dot(normed_scr[rows, :], hidden_w[...]) + as_row(hidden_b)
        square = hidden * hidden
        bend = 0.7978845608028654 * 0.044715
        curve = jnp.tanh(hidden * (0.7978845608028654 + bend * square))
        half = 0.5 + 0.5 * curve
        active = (hidden * half).astype(BF16)
        slope = half + (0.5 * hidden) * (1.0 - curve * curve) * (
            0.7978845608028654 + 3.0 * bend * square
        )
        hidden_grad = (dot_nt(grad_scr[rows, :], output_w[...]) * slope).astype(BF16)
        out_acc[rows, :] += dot(active, output_w[...])
        mid_acc[rows, :] += dot_nt(hidden_grad, hidden_w[...])
        ow_acc[:, units_of] += dot(grad_t[:, rows], active)
        hw_acc[:, units_of] += dot(normed_t[:, rows], hidden_grad)
        hb_acc[:, units_of] += column_sum(hidden_grad.astype(F32))

    @pl.when(f == SPLIT - 1)
    def _():
        for j in range(u):

            for b in range(units[j][1]):
                source = pl.ds(b * BLOCK, BLOCK)
                at = b + lows[j]
                rows = pl.ds(at * BLOCK, BLOCK)
                mods = mods_ref[at : at + 1, :]
                gate_one, scale_two, gate_two = mods[:, cut(2)], mods[:, cut(4)], mods[:, cut(5)]
                middle, branch = middle_scr[rows, :], branch_scr[rows, :]
                cot = cotangent(at)
                output = out_acc[rows, :] + as_row(output_b)
                result = (middle + gate_two * output).astype(BF16)
                for s in range(n):
                    out_ref[s, at] = result[s * chunk : (s + 1) * chunk]
                normed, inverse = layer_norm(middle)
                mid_grad = mid_acc[rows, :]
                middle_grad = cot + norm_back(mid_grad * (1.0 + scale_two), normed, inverse)
                middle_out[rows, :] = middle_grad
                branch_grad = (gate_one * middle_grad).astype(BF16)
                mw_acc[...] += dot(mixes[j][source, :].T, branch_grad)
                mb_acc[...] += column_sum(branch_grad.astype(F32))
                mixed_grad_out[rows, :] = dot_nt(branch_grad, mixer_w[...]).astype(BF16)
                found = (
                    column_sum(middle_grad * branch),
                    column_sum(mid_grad),
                    column_sum(mid_grad * normed),
                    column_sum(cot * output),
                )
                for m, row in enumerate(found):
                    slots_acc[m, at : at + 1, :] = row

        ff = ow_acc.shape[1]
        rows_scr[:ff, :] = ow_acc[...].T.astype(BF16)
        for j in range(ff // width):
            lo = ff + j * width
            rows_scr[lo : lo + width, :] = hw_acc[:, j * width : (j + 1) * width].astype(BF16)
        if rows_scr.shape[0] > 2 * ff:
            rows_scr[2 * ff :, :] = jnp.zeros((rows_scr.shape[0] - 2 * ff, width), BF16)
        spread_out(me_ref, rows_scr.shape[0] // size, size, rows_scr, (first_out, second_out))
        mixer_out[...] = mw_acc[...]
        sums = [ob_acc[...]]
        sums += [hb_acc[:, j * width : (j + 1) * width] for j in range(ff // width)]
        sums += [mb_acc[...], jnp.zeros((8 - 2 - ff // width, width), F32)]
        small = [slots_acc[m] for m in range(4)] + [activity_ref[...]] + sums
        small_out[...] = jnp.concatenate(small, axis=0).astype(BF16)


def feed(units, n, chunk, size, me, valid, xs, mixes, cots, mods, activity, weights):
    width, ff = weights[2].shape
    total = sum(count for _, count in units)
    shape = jax.ShapeDtypeStruct
    tokens, part = total * BLOCK, ff // SPLIT
    arrays = [*xs, *mixes, cots, mods, activity, *weights]
    in_specs = [full(a.shape) for a in arrays]
    in_specs[-4] = pl.BlockSpec((width, part), lambda f: (0, f))
    in_specs[-3] = pl.BlockSpec((part,), lambda f: (f,))
    in_specs[-2] = pl.BlockSpec((part, width), lambda f: (f, 0))
    rows = padded(2 * ff, size)
    outs = [shape((n, total, chunk, width), BF16)]
    outs += [shape((tokens, width), F32), shape((tokens, width), BF16)]
    outs += [shape((rows // 2, width), BF16)] * 2
    outs += [shape((width, width), F32), shape((48, width), BF16)]
    in_specs, arrays = [SMEM] + in_specs, [me] + arrays
    if valid is not None:
        in_specs, arrays = [SMEM] + in_specs, [me, valid] + arrays[1:]
    found = pl.pallas_call(
        partial(feed_kernel, units, n, chunk, width, size, valid is not None),
        grid=(SPLIT,),
        in_specs=in_specs,
        out_specs=[full(o.shape) for o in outs],
        out_shape=outs,
        scratch_shapes=[
            pltpu.VMEM((tokens, width), F32),
            pltpu.VMEM((tokens, width), F32),
            pltpu.VMEM((tokens, width), F32),
            pltpu.VMEM((tokens, width), F32),
            pltpu.VMEM((tokens, width), BF16),
            pltpu.VMEM((tokens, width), BF16),
            pltpu.VMEM((width, tokens), BF16),
            pltpu.VMEM((width, tokens), BF16),
            pltpu.VMEM((width, ff), F32),
            pltpu.VMEM((width, ff), F32),
            pltpu.VMEM((width, width), F32),
            pltpu.VMEM((1, width), F32),
            pltpu.VMEM((1, ff), F32),
            pltpu.VMEM((1, width), F32),
            pltpu.VMEM((rows, width), BF16),
            pltpu.VMEM((4, 8, width), F32),
        ],
        compiler_params=params(),
        cost_estimate=cost(0.1),
        name="feed",
    )(*arrays)
    return found[0], found[1:]


def finish_kernel(units, n, chunk, width, count, *refs):
    u = len(units)
    total = sum(c for _, c in units)
    xs, refs = refs[:u], refs[u:]
    parts, weight_ref, refs = refs[: 3 * PAIRS], refs[3 * PAIRS], refs[3 * PAIRS + 1 :]
    if u > 1:
        own_ref, others, refs = refs[0], refs[1 : 1 + count], refs[1 + count :]
    sums, refs = refs[0], refs[1:]
    middle_ref, mods_ref, out_ref, small_out, x_scr, g_scr, slots_acc = refs
    i = pl.program_id(0)

    @pl.when(i == 0)
    def _():
        slots_acc[...] = jnp.zeros_like(slots_acc)

    @pl.when(i < HALF)
    def _():
        x_scr[...] = xs[0][...]
        grads = jnp.concatenate([part[0] for part in parts], axis=1)
        g_scr[...] = dot_nt(grads, weight_ref[...])

    if u > 1:

        @pl.when(i >= HALF)
        def _():
            x_scr[...] = xs[1][...]
            grad = own_ref[...]
            for other in others:
                grad = grad + other[...].astype(F32)
            g_scr[...] = grad

    scale_one = mods_ref[pl.ds(i, 1), width : 2 * width]
    normed, inverse = layer_norm(x_scr[...].astype(F32))
    grad = g_scr[...]
    slots_acc[0, pl.ds(i, 1), :] = column_sum(grad)
    slots_acc[1, pl.ds(i, 1), :] = column_sum(grad * normed)
    result = middle_ref[...] + norm_back(grad * (1.0 + scale_one), normed, inverse)
    result = result.astype(BF16)
    for s in range(n):
        out_ref[s, 0] = result[s * chunk : (s + 1) * chunk]

    @pl.when(i == total - 1)
    def _():
        biases = [
            jnp.concatenate(
                [sums[j, 0:1, m * LANES : (m + 1) * LANES] for j in range(PAIRS)], axis=1
            )
            for m in (0, 2)
        ]
        small = [slots_acc[0], slots_acc[1], *biases, jnp.zeros((14, width), F32)]
        small_out[...] = jnp.concatenate(small, axis=0).astype(BF16)


def finish(units, n, chunk, xs, parts, weight, own, others, sums, middle, mods):
    width = middle.shape[1]
    total = sum(count for _, count in units)
    shape = jax.ShapeDtypeStruct
    lows = [sum(count for _, count in units[:j]) for j in range(len(units))]

    def rows_of(j, columns):
        return pl.BlockSpec(
            (BLOCK, columns), lambda i: (jnp.clip(i - lows[j], 0, units[j][1] - 1), 0)
        )

    in_specs = [rows_of(j, width) for j in range(len(units))]
    arrays = list(xs)
    for part in parts:
        for p in range(PAIRS):
            in_specs.append(
                pl.BlockSpec(
                    (1, BLOCK, LANES), lambda i, p=p: (p, jnp.clip(i, 0, HALF - 1), 0)
                )
            )
            arrays.append(part)
    in_specs.append(full(weight.shape))
    arrays.append(weight)
    if len(units) > 1:
        in_specs += [rows_of(1, width)] * (1 + len(others))
        arrays += [own, *others]
    in_specs += [full(sums.shape)]
    in_specs += [pl.BlockSpec((BLOCK, width), lambda i: (i, 0)), full(mods.shape)]
    arrays += [sums, middle, mods]
    return pl.pallas_call(
        partial(finish_kernel, units, n, chunk, width, len(others)),
        grid=(total,),
        in_specs=in_specs,
        out_specs=[
            pl.BlockSpec((n, 1, chunk, width), lambda i: (0, i, 0, 0)),
            full((32, width)),
        ],
        out_shape=[shape((n, total, chunk, width), BF16), shape((32, width), BF16)],
        scratch_shapes=[
            pltpu.VMEM((BLOCK, width), BF16),
            pltpu.VMEM((BLOCK, width), F32),
            pltpu.VMEM((2, 8, width), F32),
        ],
        compiler_params=params(),
        cost_estimate=cost(0.1),
        name="finish",
    )(*arrays)


def settle_kernel(size, chunk, places, kept, me_ref, *refs):
    pieces, outs, small_out, rows_scr = refs[:kept], refs[kept:-2], refs[-2], refs[-1]
    held = pieces[0].shape[0] // (size // kept)
    for j, piece in enumerate(pieces):

        @pl.loop(0, size // kept)
        def _(p, j=j, piece=piece):
            at = pl.multiple_of(((p + j * (size // kept)) ^ me_ref[0]) * chunk, chunk)
            low = pl.multiple_of(p * held, 16)
            rows_scr[pl.ds(at, chunk), :] = piece[pl.ds(low, chunk), :].astype(F32)
            small_out[p + j * (size // kept)] = piece[pl.ds(low + chunk, held - chunk), :].astype(F32)

    width = rows_scr.shape[1]
    for out, low in zip(outs, places):
        rows = out.shape[0]
        for c in range(out.shape[1] // width):
            out[:, c * width : (c + 1) * width] = rows_scr[low + c * rows : low + (c + 1) * rows, :]


def settle(size, chunk, me, pieces, shapes):
    width = pieces[0].shape[1]
    held = pieces[0].shape[0] * len(pieces) // size
    places, low = [], 0
    for rows, columns in shapes:
        places.append(low)
        low += rows * (columns // width)
    shapes = [*shapes, (size, held - chunk, width)]
    return pl.pallas_call(
        partial(settle_kernel, size, chunk, places, len(pieces)),
        in_specs=[SMEM] + [full(h.shape) for h in pieces],
        out_specs=[full(s) for s in shapes],
        out_shape=[jax.ShapeDtypeStruct(s, F32) for s in shapes],
        grid=(1,),
        scratch_shapes=[pltpu.VMEM((size * chunk, width), F32)],
        compiler_params=params(40),
        cost_estimate=cost(0.1),
        name="settle",
    )(me, *pieces)


def modulate_kernel(early_ref, late_ref, weight_out, bias_out, query_out, value_out, *outs):
    size, _, width = early_ref.shape
    mixer_out, hidden_out, output_out = outs
    flat = lambda ref, m: ref[:, 8 * m : 8 * (m + 1), :].reshape(size * 8, width)
    activity = flat(early_ref, 4).astype(BF16).T
    for m in range(6):
        slots = flat(late_ref, m) if m < 2 else flat(early_ref, m - 2)
        lanes = slice(m * width, (m + 1) * width)
        weight_out[:, lanes] = dot(activity, slots.astype(BF16))
        bias_out[lanes] = column_sum(slots).reshape(-1)
    early = jnp.sum(early_ref[:, 40:48, :], axis=0)
    late = jnp.sum(late_ref[:, 16:24, :], axis=0)
    query_out[...] = late[0:1].reshape(-1)
    value_out[...] = late[1:2].reshape(-1)
    output_out[...] = early[0:1].reshape(-1)
    parts = hidden_out.shape[0] // width
    for j in range(parts):
        hidden_out[j * width : (j + 1) * width] = early[1 + j : 2 + j].reshape(-1)
    mixer_out[...] = early[1 + parts : 2 + parts].reshape(-1)


def modulate(early, late, ff):
    width = early.shape[2]
    shapes = [(width, 6 * width), (6 * width,), (width,), (width,), (width,), (ff,), (width,)]
    return pl.pallas_call(
        modulate_kernel,
        out_shape=[jax.ShapeDtypeStruct(s, F32) for s in shapes],
        compiler_params=params(40),
        cost_estimate=cost(0.1),
        name="modulate",
    )(early, late)


def xor_permute(value, mask, size):
    return lax.ppermute(value, ("rows", "band"), [(i, i ^ mask) for i in range(size)])


def stages_of(rows, bands):
    band_bits, bits = bands.bit_length() - 1, (rows * bands).bit_length() - 1
    stages = [[band_bits]]
    for low, high in ((band_bits + 1, bits), (0, band_bits)):
        if (high - low) % 2:
            stages.append([low])
            low += 1
        stages += [[b, b + 1] for b in range(low, high, 2)]
    return stages


def digit_of(me, stage):
    return sum(((me >> b) & 1) << i for i, b in enumerate(stage))


def mask_of(t, stage):
    return sum(((t >> i) & 1) << b for i, b in enumerate(stage))


def fold_kernel(count, *refs):
    total = refs[0][...].astype(F32)
    for ref in refs[1:count]:
        total = total + ref[...].astype(F32)
    outs = refs[count:]
    rows = total.shape[0] // len(outs)
    for j, out in enumerate(outs):
        out[...] = total[j * rows : (j + 1) * rows].astype(BF16)


def fold(arrays, parts):
    rows, width = arrays[0].shape
    shape = jax.ShapeDtypeStruct((rows // parts, width), BF16)
    found = pl.pallas_call(
        partial(fold_kernel, len(arrays)),
        out_shape=[shape] * parts,
        compiler_params=params(32),
        cost_estimate=cost(0.1),
        name="fold",
    )(*arrays)
    return list(found)


def after(value, *others):
    return lax.optimization_barrier((value, others))[0]


def join_kernel(count, *refs):
    rows = refs[0].shape[0]
    for j in range(count):
        refs[count][j * rows : (j + 1) * rows, :] = refs[j][...]


def join(arrays):
    rows, width = arrays[0].shape
    return pl.pallas_call(
        partial(join_kernel, len(arrays)),
        out_shape=jax.ShapeDtypeStruct((rows * len(arrays), width), BF16),
        compiler_params=params(32),
        cost_estimate=cost(0.1),
        name="join",
    )(*arrays)


class Sum:
    def __init__(self, stages, size, parts):
        self.stages, self.size, self.at = stages, size, 0
        self.scattered = False
        self.steps = self.left = 2 * len(stages) - 1
        self.send(parts)

    def send(self, parts):
        stage = self.stages[self.at]
        self.held = [parts[0]] + [
            xor_permute(part, mask_of(t, stage), self.size) for t, part in enumerate(parts) if t
        ]

    def step(self, extra=None, done=()):
        held = list(after(self.held, *done)) if done else self.held
        self.left -= 1
        self.at += -1 if self.scattered else 1
        if not self.scattered and self.at < len(self.stages):
            parts = fold(held, 1 << len(self.stages[self.at]))
            self.send(parts)
            return parts
        if not self.scattered:
            self.scattered = True
            self.at -= 1
            value = fold(held, 1)[0]
            if extra is not None:
                value = jnp.concatenate([value, extra], axis=0)
        else:
            value = join(held)
        self.send([value] * (1 << len(self.stages[self.at])))
        return [value]


def body(
    patches,
    condition_table,
    condition_index,
    image_lengths,
    modulate_weight,
    modulate_bias,
    triple_weight,
    query_bias,
    value_bias,
    mixer_weight,
    mixer_bias,
    hidden_weight,
    hidden_bias,
    output_weight,
    output_bias,
    cotangent,
):
    band = lax.axis_index("band")
    n = lax.axis_size("band")
    size = n * lax.axis_size("rows")
    everyone = lax.axis_index(("rows", "band"))
    rows, band_length, width = patches.shape
    ff = hidden_weight.shape[1]
    length = band_length * n
    big = length // 2
    chunk = band_length // (2 * HALF)
    assert length == 2 * HALF * BLOCK
    plan = Plan(rows, n)
    units, total = plan.units(), plan.total
    assert units[0][1] == HALF
    stages = stages_of(size // n, n)
    relative = jnp.int32(0)
    for stage in stages:
        relative = (relative << len(stage)) | digit_of(everyone, stage)
    relative = relative.astype(jnp.int32).reshape(1)

    def deal(pieces):
        return lax.all_to_all(pieces, "band", 0, 0, tiled=True)

    me = band.astype(jnp.int32).reshape(1)
    packed = pack(plan, chunk, big, me, image_lengths, patches, True)
    x_pieces = [p if s == 0 else xor_permute(p, s, size) for s, p in enumerate(packed)]

    mods, activity, flags = prepare(
        plan,
        big,
        me,
        image_lengths,
        condition_index,
        condition_table,
        modulate_weight,
        modulate_bias,
    )
    c_packed = pack(plan, chunk, big, me, image_lengths, after(cotangent, packed), False)
    c_pieces = deal(after(c_packed, mods, x_pieces[1:TIE]))

    attended, xs, mixes = [], [], []
    others = [[] for _ in units]
    if plan.group > 1:
        own = collect(n, plan.whole * HALF, plan.own, chunk, me, x_pieces)
        others[-1] = [xor_permute(own, t, size) for t in range(1, plan.group)]
    for j, (name, count) in enumerate(units):
        lo = j * HALF
        found = attend(
            n,
            j,
            lo,
            count,
            HALF,
            chunk,
            me,
            flags,
            x_pieces,
            others[j],
            mods,
            triple_weight,
            query_bias,
            value_bias,
        )
        xs.append(found[0])
        attended.append(found[1:8])
        mixes.append(found[8])

    valid = None
    if plan.idle:
        valid = (plan.half_row("shared", band) < plan.halves).astype(F32).reshape(1)

    weights = [
        mixer_weight,
        mixer_bias,
        hidden_weight,
        hidden_bias,
        output_weight,
        output_bias,
    ]
    out_pieces, fed = feed(
        units,
        n,
        chunk,
        size,
        relative,
        valid,
        xs,
        mixes,
        c_pieces,
        mods,
        activity,
        weights,
    )
    middle_grad, mixed_grad, first, second, mixer_grad, feed_small = fed
    out_back = deal(out_pieces)
    feed_sum = Sum(stages, size, [first, second])

    own, others, begun = None, [], []
    token = feed_sum.step()
    mixed_grad = after(mixed_grad, *token)
    if len(units) > 1:
        kept, low = attended[1], HALF
        found = shared_back(units[1][1], HALF, flags, kept, mixed_grad, low, triple_weight)
        own, others = found[0], [xor_permute(o, t + 1, size) for t, o in enumerate(found[1:-2])]
        begun = found[-2:]
        token = feed_sum.step(feed_small, done=(own,))
    grad = after(mixed_grad, *token)
    *parts, sums, first, second = whole_back(
        size, relative, flags, attended[0], grad, begun, mixer_grad
    )
    token = feed_sum.step(feed_small, done=(sums,))
    grad_pieces, last_small = finish(
        units,
        n,
        chunk,
        xs,
        parts,
        triple_weight,
        own,
        others,
        sums,
        after(middle_grad, out_back, *token),
        mods,
    )
    feed_chunk, last_chunk = (padded(r, size) // size for r in (2 * ff, 4 * width))
    last_sum = Sum(stages, size, after([first, second], last_small))
    spreading = feed_sum.step(feed_small, done=(last_small,))
    grad_back = deal(after(grad_pieces, spreading))
    for _ in range(3):
        last_sum.step(last_small)
    token = last_sum.step(last_small, done=(grad_back,))
    while feed_sum.left:
        feed_sum.step(feed_small, done=token)
        if last_sum.left > 1:
            token = last_sum.step(last_small)
    block_out = unpack(plan, chunk, big, image_lengths, out_back, BF16)
    output_w_grad, hidden_w_grad, early = settle(
        size, feed_chunk, relative, feed_sum.held, [(ff, width), (width, ff)]
    )
    patch_grad = unpack(plan, chunk, big, image_lengths, grad_back, F32)
    while last_sum.left:
        token = ()
        if last_sum.left == 1:
            token = (patch_grad, block_out)
        last_sum.step(last_small, done=token)
    triple_w_grad, mixer_w_grad, late = settle(
        size, last_chunk, relative, last_sum.held, [(width, 3 * width), (width, width)]
    )
    modulate_w_grad, modulate_b_grad, query_b, value_b, mixer_b, hidden_b, output_b = modulate(
        early, late, ff
    )
    return (
        block_out,
        patch_grad,
        modulate_w_grad,
        modulate_b_grad,
        triple_w_grad,
        query_b,
        value_b,
        mixer_w_grad,
        mixer_b,
        hidden_w_grad,
        hidden_b,
        output_w_grad,
        output_b,
    )


def solution(mesh):
    return jax.shard_map(
        body,
        mesh=mesh,
        in_specs=(
            P("rows", None, "band"),
            P(),
            P("rows", None),
            P("rows", None),
            P(),
            P(),
            P(),
            P(),
            P(),
            P(),
            P(),
            P(),
            P(),
            P(),
            P(),
            P("rows", None, "band"),
        ),
        out_specs=(
            P("rows", None, "band"),
            P("rows", None, "band"),
            P(),
            P(),
            P(),
            P(),
            P(),
            P(),
            P(),
            P(),
            P(),
            P(),
            P(),
        ),
        check_vma=False,
    )
```
